256 devices in a mesh: ctx: 32 (over y_lo, z, core), tp: 8 (over x, y_hi).
Axes of the slice: x: 4, y: 4 (y_hi: 2, y_lo: 2; y = y_hi * 2 + y_lo), z: 8, core: 2. Of those that a mesh axis runs over, the one named last changes fastest.
Arguments:
- tokens: bfloat16 [8192, 5120], P('ctx', 'tp'), may hold values from -6 to 6
- qkv_weight: bfloat16 [5120, 3, 3072], P(None, None, 'tp')
- query_gain: float32 [3072], P('tp'), may hold values from 0.5 to 1.25
- key_gain: float32 [3072], P('tp'), may hold values from 0.5 to 1.25
- out_weight: bfloat16 [3072, 5120], P('tp', 'ctx'), may hold values from -0.109375 to 0.109375
- block_ids: int32 [8192], P('ctx'), may hold values from 0 to 31, as said below
Outputs:
- mixed_out: bfloat16 [8192, 5120], P('ctx', 'tp')
The draws below stay inside these ranges and needn't reach their ends.
Inputs may be any that keep to these rules, and one draw needn't show every extreme that they name: `block_ids`: the 256 tokens of each index of ctx form one frame span and share one span number; the span numbers of the 32 indices are a permutation of 0 to 31.
All inputs are finite; a program needn't handle non-finite values.
Results may differ from the reference program's by a relative error of at most 0.017.
Values may be sent and summed in bfloat16 or wider, within the bound.
No kernel may reach another device: no remote copies, remote signals or barrier semaphores. Data moves between devices by JAX's collectives and lax.ppermute only.
A program may use at most 128 MiB of HBM per device.

```python
import math
import jax
import jax.numpy as jnp
from jax import lax

D = 5120
HEADS = 24
HD = 128
TOK_DEV = 256
TOKENS = 8192
N_CTX = 32
N_TP = 8


def draw_block_ids(key, part):
    key = jax.random.fold_in(key, 11)
    order = jax.random.permutation(key, N_CTX).astype(jnp.int32)
    return jnp.broadcast_to(order[:, None], (N_CTX, TOK_DEV)).reshape(N_CTX * TOK_DEV)


def draw_qkv_weight(key, part):
    key = jax.random.fold_in(key, 23)
    first_key, second_key = jax.random.split(key)
    width = HEADS * HD
    base = jax.random.normal(first_key, (D, 3, width), jnp.float32) * D ** (-0.5)
    place = jnp.arange(width, dtype=jnp.float32) / (width - 1)
    column_scale = 3.0 ** place * jax.random.uniform(second_key, (width,), jnp.float32, 0.8, 1.25)
    return (base * column_scale[None, None, :]).astype(jnp.bfloat16)


def steps_of(key, shape, shards, low, top_value):
    level = 1.0
    for dim, blocks in shards:
        draws = jax.random.uniform(jax.random.fold_in(jax.random.fold_in(key, 6), dim), (blocks,), jnp.float32, low / len(shards), top_value / len(shards))
        level = level * jnp.repeat(jnp.exp(draws), shape[dim] // blocks).reshape((-1,) + (1,) * (len(shape) - 1 - dim))
    return level


def centred(own_key, extent, spread, limit, pieces=(), held_as=jnp.bfloat16):
    loudness = steps_of(own_key, extent, pieces, -0.22, 0.18) if pieces else 1.0
    entries = jax.random.normal(own_key, extent, jnp.float32) * spread * loudness
    return jnp.minimum(jnp.maximum(entries, -limit), limit).astype(held_as)


def setup_inputs(seed: int = 0) -> dict:
    seeds = jax.random.split(jax.random.key(seed), 7)
    return {
        "tokens": centred(seeds[0], (TOKENS, D), 1.0, 6.0, ((0, 32), (1, 8))),
        "qkv_weight": draw_qkv_weight(jax.random.fold_in(seeds[6], 71), 0),
        "query_gain": jnp.clip(jnp.exp(math.log(1.25) - 0.916290732 * jax.random.uniform(seeds[2], (HEADS * HD,), jnp.float32) ** steps_of(seeds[2], (HEADS * HD,), ((0, 8),), -0.2, 0.2)), 0.5, 1.25),
        "key_gain": jnp.clip(jnp.exp(math.log(1.25) - 0.916290732 * jax.random.uniform(seeds[3], (HEADS * HD,), jnp.float32) ** steps_of(seeds[3], (HEADS * HD,), ((0, 8),), -0.2, 0.2)), 0.5, 1.25),
        "out_weight": centred(seeds[4], (HEADS * HD, D), (HEADS * HD) ** -0.5, 0.109375, ((0, 8), (1, 32))),
        "block_ids": draw_block_ids(jax.random.fold_in(seeds[6], 71), 0),
    }


def full_norm(flat_part, gain_vector):
    inverse = lax.rsqrt(lax.optimization_barrier(jnp.mean(flat_part * flat_part, axis=-1, keepdims=True)) + 1e-06)
    normed = (flat_part * inverse * gain_vector).astype(jnp.bfloat16)
    return normed.reshape(flat_part.shape[0], HEADS, HD)

def reference(tokens, qkv_weight, query_gain, key_gain, out_weight, block_ids):
    flat = jnp.dot(tokens, qkv_weight.reshape(D, 3 * HEADS * HD), preferred_element_type=jnp.float32)
    flat = flat.reshape(TOKENS, 3, HEADS * HD)
    queries = full_norm(flat[:, 0], query_gain)
    keys = full_norm(flat[:, 1], key_gain)
    values = flat[:, 2].astype(jnp.bfloat16).reshape(TOKENS, HEADS, HD)
    block_count = TOKENS // TOK_DEV
    query_groups = block_ids.reshape(block_count, TOK_DEV)

    def one_head(operands):
        query_head, key_head, value_head = operands

        def one_block(block_operands):
            query_block, group_ids = block_operands
            scores = jnp.dot(query_block, key_head.T, preferred_element_type=jnp.float32) * (1.0 / math.sqrt(HD))
            weights = jnp.where(block_ids[None, :] <= group_ids[:, None], jnp.exp(scores), 0.0)
            totals = lax.optimization_barrier(jnp.sum(weights, axis=1))
            accum = jnp.dot(weights.astype(jnp.bfloat16), value_head, preferred_element_type=jnp.float32)
            return (accum / totals[:, None]).astype(jnp.bfloat16)
        blocks_out = lax.map(one_block, (query_head.reshape(block_count, TOK_DEV, HD), query_groups))
        return blocks_out.reshape(TOKENS, HD)
    heads_out = lax.map(one_head, (queries.transpose(1, 0, 2), keys.transpose(1, 0, 2), values.transpose(1, 0, 2)))
    attention = heads_out.transpose(1, 0, 2).reshape(TOKENS, HEADS * HD)
    group_width = HEADS * HD // N_TP
    summed = jnp.zeros((TOKENS, D), jnp.float32)
    for group in range(N_TP):
        part_term = jnp.dot(attention[:, group * group_width:(group + 1) * group_width], out_weight[group * group_width:(group + 1) * group_width], preferred_element_type=jnp.float32)
        rounded = lax.optimization_barrier(part_term.astype(jnp.bfloat16))
        summed = summed + rounded.astype(jnp.float32)
    return summed.astype(jnp.bfloat16)
```

```python
import math

import jax
import jax.numpy as jnp
from jax import lax
from jax.experimental import pallas as pl
from jax.experimental.pallas import tpu as pltpu
from jax.sharding import PartitionSpec as P

HEADS = 24
HD = 128
ID_ROWS = 16
N_Z = 8
N_X = 4
N_TP = 8
N_CTX = 32
MIB = 1 << 20


def move(value, x=0, y_hi=0, y_lo=0, z=0, core=0):
    pairs = []
    for c in range(N_CTX):
        for t in range(N_TP):
            c_lo, c_z, c_core = c // 16, (c // 2) % 8, c % 2
            t_x, t_hi = t // 2, t % 2
            dst_c = ((c_lo + y_lo) % 2) * 16 + ((c_z + z) % N_Z) * 2 + (c_core + core) % 2
            dst_t = ((t_x + x) % N_X) * 2 + (t_hi + y_hi) % 2
            pairs.append((c * N_TP + t, dst_c * N_TP + dst_t))
    return lax.ppermute(value, ("ctx", "tp"), pairs)


TP_STEPS = [(0, 0), (0, 1), (1, 0), (3, 0), (1, 1), (3, 1), (2, 0), (2, 1)]


def gather_tp(value):
    blocks = [value]
    for x, y_hi in TP_STEPS[1:]:
        blocks.append(None)
    for r in (7, 6, 5, 4, 3, 2, 1):
        x, y_hi = TP_STEPS[r]
        blocks[r] = move(value, x=x, y_hi=y_hi)
    return blocks


def sender_places():
    t = lax.axis_index("tp")
    t_x, t_hi = t // 2, t % 2
    return jnp.stack(
        [((t_x - x + N_X) % N_X) * 2 + (t_hi - y_hi + 2) % 2 for x, y_hi in TP_STEPS]
    ).astype(jnp.int32)


def qkv_kernel(place_ref, *refs):
    toks, (w_ref, q_ref, k_ref, v_ref, sq_ref, acc_ref) = refs[:8], refs[8:]
    step = pl.program_id(0)
    for r in range(8):

        @pl.when(step == r)
        def _():
            for p in range(3):
                term = jnp.dot(toks[r][...], w_ref[p], preferred_element_type=jnp.float32)
                acc_ref[p] = term if r == 0 else acc_ref[p] + term

    @pl.when(step == 7)
    def _():
        q, k = acc_ref[0], acc_ref[1]
        q_ref[...] = q
        k_ref[...] = k
        v_ref[...] = acc_ref[2].astype(jnp.bfloat16)
        q_sq = jnp.sum(q * q, axis=1, keepdims=True)
        k_sq = jnp.sum(k * k, axis=1, keepdims=True)
        lane = lax.broadcasted_iota(jnp.int32, (q.shape[0], 128), 1)
        both = jnp.where(lane == 0, q_sq, jnp.where(lane == 1, k_sq, 0.0))
        sq_ref[...] = both.T[:8]


def qkv(blocks, weight, places):
    rows, feats = blocks[0].shape
    width = weight.shape[2]
    whole = lambda i, place: (0, 0)
    return pl.pallas_call(
        qkv_kernel,
        grid_spec=pltpu.PrefetchScalarGridSpec(
            num_scalar_prefetch=1,
            grid=(8,),
            in_specs=[pl.BlockSpec((rows, feats), whole)] * 8
            + [pl.BlockSpec((3, feats, width), lambda i, place: (0, place[i], 0))],
            out_specs=[pl.BlockSpec((rows, width), whole)] * 3 + [pl.BlockSpec((8, rows), whole)],
            scratch_shapes=[pltpu.VMEM((3, rows, width), jnp.float32)],
        ),
        out_shape=[
            jax.ShapeDtypeStruct((rows, width), jnp.float32),
            jax.ShapeDtypeStruct((rows, width), jnp.float32),
            jax.ShapeDtypeStruct((rows, width), jnp.bfloat16),
            jax.ShapeDtypeStruct((8, rows), jnp.float32),
        ],
        compiler_params=pltpu.CompilerParams(vmem_limit_bytes=24 * MIB),
        cost_estimate=pl.CostEstimate(
            flops=2 * rows * 8 * feats * 3 * width, bytes_accessed=8 * feats * 3 * width * 2, transcendentals=0
        ),
        name="qkv",
    )(places, *blocks, weight)


def norm_kernel(id_ref, s0, s1, s2, s3, q_ref, k_ref, qg_ref, kg_ref, q_out, k_out):
    rows = q_ref.shape[0]
    total = s0[...] + s1[...] + s2[...] + s3[...]
    inverse = lax.rsqrt(total * (1.0 / (HEADS * HD)) + 1e-06)
    columns = jnp.concatenate([inverse, jnp.zeros((120, rows), jnp.float32)], axis=0).T
    q_scale = math.log2(math.e) / math.sqrt(HD)
    q_out[:rows] = (q_ref[...] * columns[:, 0:1] * (qg_ref[...] * q_scale)).astype(jnp.bfloat16)
    k_out[:rows] = (k_ref[...] * columns[:, 1:2] * kg_ref[...]).astype(jnp.bfloat16)
    span = jnp.full((ID_ROWS, q_ref.shape[1]), id_ref[0].astype(jnp.float32), jnp.float32)
    q_out[rows:] = span.astype(jnp.bfloat16)
    k_out[rows:] = span.astype(jnp.bfloat16)


def norm(span_id, squares, q, k, q_gain, k_gain):
    rows, width = q.shape
    vmem = pl.BlockSpec(memory_space=pltpu.VMEM)
    out = jax.ShapeDtypeStruct((rows + ID_ROWS, width), jnp.bfloat16)
    return pl.pallas_call(
        norm_kernel,
        in_specs=[pl.BlockSpec(memory_space=pltpu.SMEM)] + [vmem] * 8,
        out_specs=[vmem] * 2,
        out_shape=[out, out],
        compiler_params=pltpu.CompilerParams(vmem_limit_bytes=12 * MIB),
        name="norm",
    )(span_id, *squares, q, k, q_gain, k_gain)


def attend_kernel(n_keys, first, last, *refs):
    qs, ks, vs = refs[:4], refs[4 : 4 + n_keys], refs[4 + n_keys : 4 + 2 * n_keys]
    rest = refs[4 + 2 * n_keys :]
    rows = vs[0].shape[0]
    heads = vs[0].shape[1] // HD
    if first:
        acc_ref, = rest[:1]
        acc_ref[...] = jnp.zeros_like(acc_ref)
    elif last:
        acc_in, keep_ref, send_ref, acc_ref = rest
        acc_ref[...] = acc_in[...]
    else:
        acc_in, acc_ref = rest
        acc_ref[...] = acc_in[...]
    lane = lax.broadcasted_iota(jnp.int32, (rows, HD), 1)
    ones = jnp.ones((rows, HD), jnp.bfloat16)
    q_ids = [jnp.max(q[rows:, :HD].astype(jnp.float32)) for q in qs]
    k_ids = [jnp.max(k[rows:, :HD].astype(jnp.float32)) for k in ks]
    for i in range(4):
        for j in range(n_keys):

            @pl.when(k_ids[j] <= q_ids[i])
            def _():
                sums = None
                for h in range(heads):
                    cols = slice(h * HD, (h + 1) * HD)
                    scores = lax.dot_general(
                        qs[i][:rows, cols], ks[j][:rows, cols], (((1,), (1,)), ((), ())),
                        preferred_element_type=jnp.float32,
                    )
                    weights = jnp.exp2(scores).astype(jnp.bfloat16)
                    wide = jnp.concatenate([vs[j][:, cols], ones], axis=1)
                    both = jnp.dot(weights, wide, preferred_element_type=jnp.float32)
                    acc_ref[i, :, cols] += both[:, :HD]
                    sums = both[:, HD:] if h == 0 else jnp.where(lane == h, both[:, HD:], sums)
                acc_ref[i, :, heads * HD :] += sums
    if last:
        for n, i in enumerate((0, 2)):
            keep_ref[n] = acc_ref[i]
        for n, i in enumerate((1, 3)):
            send_ref[n] = acc_ref[i].astype(jnp.bfloat16)


def attend(qs, ks, vs, state, last):
    rows, width = vs[0].shape
    n_keys = len(ks)
    wide = width + HD
    vmem = pl.BlockSpec(memory_space=pltpu.VMEM)
    state_shape = jax.ShapeDtypeStruct((4, rows, wide), jnp.float32)
    if last:
        out_shape = [
            jax.ShapeDtypeStruct((2, rows, wide), jnp.float32),
            jax.ShapeDtypeStruct((2, rows, wide), jnp.bfloat16),
        ]
        scratch = [pltpu.VMEM((4, rows, wide), jnp.float32)]
    else:
        out_shape, scratch = [state_shape], []
    first = state is None
    args = [*qs, *ks, *vs] + ([] if first else [state])

    def body(*refs):
        attend_kernel(n_keys, first, last, *refs)

    flops = 4 * n_keys * 3 * rows * rows * HD * 4
    return pl.pallas_call(
        body,
        in_specs=[vmem] * len(args),
        out_specs=[vmem] * len(out_shape),
        out_shape=out_shape,
        scratch_shapes=scratch,
        compiler_params=pltpu.CompilerParams(vmem_limit_bytes=32 * MIB),
        cost_estimate=pl.CostEstimate(
            flops=flops, bytes_accessed=8 * MIB, transcendentals=4 * n_keys * 3 * rows * rows
        ),
        name="attend",
    )(*args)


def fold_kernel(keep_ref, got_ref, own_ref, send_ref):
    own_ref[...] = keep_ref[0] + got_ref[0].astype(jnp.float32)
    send_ref[...] = (keep_ref[1] + got_ref[1].astype(jnp.float32)).astype(jnp.bfloat16)


def fold(keep, got):
    _, rows, wide = keep.shape
    vmem = pl.BlockSpec(memory_space=pltpu.VMEM)
    return pl.pallas_call(
        fold_kernel,
        in_specs=[vmem] * 2,
        out_specs=[vmem] * 2,
        out_shape=[
            jax.ShapeDtypeStruct((rows, wide), jnp.float32),
            jax.ShapeDtypeStruct((rows, wide), jnp.bfloat16),
        ],
        name="fold",
    )(keep, got)


def finish_kernel(own_ref, got_ref, out_ref):
    total = own_ref[...] + got_ref[...].astype(jnp.float32)
    width = out_ref.shape[1]
    for h in range(width // HD):
        cols = slice(h * HD, (h + 1) * HD)
        out_ref[:, cols] = (total[:, cols] / total[:, width + h : width + h + 1]).astype(jnp.bfloat16)


def finish(own, got):
    rows, wide = own.shape
    vmem = pl.BlockSpec(memory_space=pltpu.VMEM)
    return pl.pallas_call(
        finish_kernel,
        in_specs=[vmem] * 2,
        out_specs=vmem,
        out_shape=jax.ShapeDtypeStruct((rows, wide - HD), jnp.bfloat16),
        name="finish",
    )(own, got)


def project_kernel(place_ref, *refs):
    blocks, (w_ref, out_ref, acc_ref) = refs[:8], refs[8:]
    step = pl.program_id(0)
    for r in range(8):

        @pl.when(step == r)
        def _():
            term = lax.dot_general(
                blocks[r][...], w_ref[0], (((1,), (1,)), ((), ())), preferred_element_type=jnp.float32
            )
            acc_ref[...] = term if r == 0 else acc_ref[...] + term

    @pl.when(step == 7)
    def _():
        out_ref[...] = acc_ref[...].astype(jnp.bfloat16)


def project(blocks, weight, places):
    rows, width = blocks[0].shape
    columns = weight.shape[1]
    whole = lambda i, place: (0, 0)
    return pl.pallas_call(
        project_kernel,
        grid_spec=pltpu.PrefetchScalarGridSpec(
            num_scalar_prefetch=1,
            grid=(8,),
            in_specs=[pl.BlockSpec((rows, width), whole)] * 8
            + [pl.BlockSpec((1, columns, width), lambda i, place: (place[i], 0, 0))],
            out_specs=pl.BlockSpec((rows, columns), whole),
            scratch_shapes=[pltpu.VMEM((rows, columns), jnp.float32)],
        ),
        out_shape=jax.ShapeDtypeStruct((rows, columns), jnp.bfloat16),
        compiler_params=pltpu.CompilerParams(vmem_limit_bytes=16 * MIB),
        cost_estimate=pl.CostEstimate(
            flops=2 * rows * 8 * width * columns, bytes_accessed=8 * width * columns * 2, transcendentals=0
        ),
        name="project",
    )(places, *blocks, weight)


def spread_weight(out_weight):
    pairs = []
    for c in range(N_CTX):
        for t in range(N_TP):
            pairs.append(((4 * t + c % 4) * N_TP + c // 4, c * N_TP + t))
    turned = lax.ppermute(out_weight.T, ("ctx", "tp"), pairs)
    columns, width = turned.shape
    whole = lax.all_gather(turned, "ctx", axis=0, tiled=True)
    return whole.reshape(N_TP, 4 * columns, width)


def on_device(tokens, qkv_weight, query_gain, key_gain, out_weight, block_ids):
    places = sender_places()
    out_whole = spread_weight(out_weight)
    q_flat, k_flat, values, squares = qkv(gather_tp(tokens), qkv_weight.transpose(1, 0, 2), places)

    pair_sum = squares + move(squares, y_hi=1)
    parts = [pair_sum] + [move(pair_sum, x=x) for x in (2, 1, 3)]
    queries, keys = norm(
        block_ids[:1], parts, q_flat, k_flat, query_gain.reshape(1, -1), key_gain.reshape(1, -1)
    )

    mate = move(queries, core=1)
    across = move(queries, y_lo=1)
    qs = [queries, mate, across, move(across, core=1)]

    k_up, k_down, v_up, v_down = [keys], [keys], [values], [values]
    for _ in range(3):
        v_up.append(move(v_up[-1], z=1))
        v_down.append(move(v_down[-1], z=-1))
        k_up.append(move(k_up[-1], z=1))
        k_down.append(move(k_down[-1], z=-1))
    k_far = move(k_up[-1], z=1)
    v_far = move(v_down[-1], z=-1)

    (state,) = attend(qs, [keys, k_up[1], k_down[1]], [values, v_up[1], v_down[1]], None, False)
    (state,) = attend(qs, [k_up[2], k_down[2]], [v_up[2], v_down[2]], state, False)
    keep, send = attend(qs, [k_up[3], k_down[3], k_far], [v_up[3], v_down[3], v_far], state, True)

    own, send = fold(keep, move(send, core=1))
    attention = finish(own, move(send, y_lo=1))
    return project(gather_tp(attention), out_whole, places)


def solution(mesh):
    in_specs = (P("ctx", "tp"), P(None, None, "tp"), P("tp"), P("tp"), P("tp", "ctx"), P("ctx"))
    out_specs = P("ctx", "tp")
    return jax.shard_map(
        on_device, mesh=mesh, in_specs=in_specs, out_specs=out_specs, check_vma=False
    )
```

```python
import math

import jax
import jax.numpy as jnp
from jax import lax
from jax.experimental import pallas as pl
from jax.experimental.pallas import tpu as pltpu
from jax.sharding import PartitionSpec as P

HEADS = 24
HD = 128
ID_ROWS = 16
N_Z = 8
N_X = 4
N_TP = 8
N_CTX = 32
MIB = 1 << 20


def move(value, x=0, y_hi=0, y_lo=0, z=0, core=0):
    pairs = []
    for c in range(N_CTX):
        for t in range(N_TP):
            c_lo, c_z, c_core = c // 16, (c // 2) % 8, c % 2
            t_x, t_hi = t // 2, t % 2
            dst_c = ((c_lo + y_lo) % 2) * 16 + ((c_z + z) % N_Z) * 2 + (c_core + core) % 2
            dst_t = ((t_x + x) % N_X) * 2 + (t_hi + y_hi) % 2
            pairs.append((c * N_TP + t, dst_c * N_TP + dst_t))
    return lax.ppermute(value, ("ctx", "tp"), pairs)


TP_STEPS = [(0, 0), (0, 1), (1, 0), (3, 0), (1, 1), (3, 1), (2, 0), (2, 1)]


def after(value, *others):
    return lax.optimization_barrier((value, *others))[0]


def gather_tp(value):
    return gather_tp_and_ring(value, None)[0]


def gather_tp_and_ring(value, block):
    send = lambda r, *ties: move(
        after(value, *ties) if ties else value, x=TP_STEPS[r][0], y_hi=TP_STEPS[r][1]
    )
    b1, b2, b3 = send(1), send(2), send(3)
    if block is None:
        b4, b5 = send(4, b1, b3), send(5, b2, b3)
        return [value, b1, b2, b3, b4, b5, send(6, b4), send(7, b5)], None
    b4, b5 = send(4, b1, b3), send(5, b2, b3, block)
    below, above = move(block, z=1), move(block, z=-1)
    b6, b7 = send(6, b4, below, above), send(7, b5, below, above)
    three = jnp.stack([block, below, above])
    ring = [three, move(three, z=3), move(three[:2], z=-3)]
    return [value, b1, b2, b3, b4, b5, b6, b7], ring


def sender_places():
    t = lax.axis_index("tp")
    t_x, t_hi = t // 2, t % 2
    return jnp.stack(
        [((t_x - x + N_X) % N_X) * 2 + (t_hi - y_hi + 2) % 2 for x, y_hi in TP_STEPS]
    ).astype(jnp.int32)


def order_kernel(place_ref, w_ref, out_ref, sems):
    feats = out_ref.shape[1] // 8

    def fetch(r):
        start = pl.multiple_of(place_ref[r] * feats, feats)
        return pltpu.make_async_copy(
            w_ref.at[:, pl.ds(start, feats), :], out_ref.at[:, pl.ds(r * feats, feats), :], sems.at[r]
        )

    for r in range(8):
        fetch(r).start()
    for r in range(8):
        fetch(r).wait()


def order_weight(weight, places):
    return pl.pallas_call(
        order_kernel,
        in_specs=[pl.BlockSpec(memory_space=pltpu.SMEM), pl.BlockSpec(memory_space=pl.ANY)],
        out_specs=pl.BlockSpec(memory_space=pltpu.VMEM),
        out_shape=jax.ShapeDtypeStruct(weight.shape, weight.dtype),
        scratch_shapes=[pltpu.SemaphoreType.DMA((8,))],
        compiler_params=pltpu.CompilerParams(vmem_limit_bytes=32 * MIB),
        cost_estimate=pl.CostEstimate(flops=0, bytes_accessed=24 * MIB, transcendentals=0),
        name="order",
    )(places, weight)


def qkv_kernel(n, low, first, last, *refs):
    toks, refs = refs[:n], refs[n:]
    acc_in, refs = (None, refs) if first else (refs[0], refs[1:])
    w_ref, outs = refs[0], refs[1:]
    feats = toks[0].shape[1]
    wide = jnp.concatenate([tok[...] for tok in toks], axis=1)
    sums = []
    for p in range(3):
        rows = slice(low * feats, (low + n) * feats)
        term = jnp.dot(wide, w_ref[p, rows, :], preferred_element_type=jnp.float32)
        if not first:
            term = acc_in[p] + term
        if not last:
            outs[0][p] = term
        sums.append(term)
    if not last:
        return
    q, k, v = sums
    q_ref, k_ref, v_ref, sq_ref = outs
    q_ref[...] = q
    k_ref[...] = k
    v_ref[...] = v.astype(jnp.bfloat16)
    q_sq = jnp.sum(q * q, axis=1, keepdims=True)
    k_sq = jnp.sum(k * k, axis=1, keepdims=True)
    lane = lax.broadcasted_iota(jnp.int32, (q.shape[0], 128), 1)
    both = jnp.where(lane == 0, q_sq, jnp.where(lane == 1, k_sq, 0.0))
    sq_ref[...] = both.T[:8]


def qkv_part(blocks, low, weight, acc):
    n = len(blocks)
    rows, feats = blocks[0].shape
    width = weight.shape[2]
    first, last = acc is None, low + n == 8
    vmem = pl.BlockSpec(memory_space=pltpu.VMEM)
    args = [*blocks] + ([] if first else [acc]) + [weight]
    if last:
        out_shape = [
            jax.ShapeDtypeStruct((rows, width), jnp.float32),
            jax.ShapeDtypeStruct((rows, width), jnp.float32),
            jax.ShapeDtypeStruct((rows, width), jnp.bfloat16),
            jax.ShapeDtypeStruct((8, rows), jnp.float32),
        ]
    else:
        out_shape = [jax.ShapeDtypeStruct((3, rows, width), jnp.float32)]

    def body(*refs):
        qkv_kernel(n, low, first, last, *refs)

    return pl.pallas_call(
        body,
        in_specs=[vmem] * len(args),
        out_specs=[vmem] * len(out_shape),
        out_shape=out_shape,
        compiler_params=pltpu.CompilerParams(vmem_limit_bytes=32 * MIB),
        cost_estimate=pl.CostEstimate(
            flops=2 * rows * n * feats * 3 * width, bytes_accessed=n * feats * 3 * width * 2, transcendentals=0
        ),
        name="qkv",
    )(*args)


def norm_kernel(id_ref, s0, s1, s2, s3, q_ref, k_ref, qg_ref, kg_ref, q_out, k_out):
    rows = q_ref.shape[0]
    total = s0[...] + s1[...] + s2[...] + s3[...]
    inverse = lax.rsqrt(total * (1.0 / (HEADS * HD)) + 1e-06)
    columns = jnp.concatenate([inverse, jnp.zeros((120, rows), jnp.float32)], axis=0).T
    q_scale = math.log2(math.e) / math.sqrt(HD)
    q_out[:rows] = (q_ref[...] * columns[:, 0:1] * (qg_ref[...] * q_scale)).astype(jnp.bfloat16)
    k_out[:rows] = (k_ref[...] * columns[:, 1:2] * kg_ref[...]).astype(jnp.bfloat16)
    span = jnp.full((ID_ROWS, q_ref.shape[1]), id_ref[0].astype(jnp.float32), jnp.float32)
    q_out[rows:] = span.astype(jnp.bfloat16)
    k_out[rows:] = span.astype(jnp.bfloat16)


def norm(span_id, squares, q, k, q_gain, k_gain):
    rows, width = q.shape
    vmem = pl.BlockSpec(memory_space=pltpu.VMEM)
    out = jax.ShapeDtypeStruct((rows + ID_ROWS, width), jnp.bfloat16)
    return pl.pallas_call(
        norm_kernel,
        in_specs=[pl.BlockSpec(memory_space=pltpu.SMEM)] + [vmem] * 8,
        out_specs=[vmem] * 2,
        out_shape=[out, out],
        compiler_params=pltpu.CompilerParams(vmem_limit_bytes=12 * MIB),
        name="norm",
    )(span_id, *squares, q, k, q_gain, k_gain)


def attend_kernel(n_keys, first, last, *refs):
    qs, ks, vs = refs[:4], refs[4 : 4 + n_keys], refs[4 + n_keys : 4 + 2 * n_keys]
    rest = refs[4 + 2 * n_keys :]
    rows = vs[0].shape[0]
    heads = vs[0].shape[1] // HD
    if first:
        acc_ref, = rest[:1]
        acc_ref[...] = jnp.zeros_like(acc_ref)
    elif last:
        acc_in, keep_ref, keep_sum, send_ref, acc_ref = rest
        acc_ref[...] = acc_in[...]
    else:
        acc_in, acc_ref = rest
        acc_ref[...] = acc_in[...]
    lane = lax.broadcasted_iota(jnp.int32, (rows, HD), 1)
    ones = jnp.ones((rows, HD), jnp.bfloat16)
    q_ids = [jnp.max(q[rows:, :HD].astype(jnp.float32)) for q in qs]
    k_ids = [jnp.max(k[rows:, :HD].astype(jnp.float32)) for k in ks]
    for i in range(4):
        for j in range(n_keys):

            @pl.when(k_ids[j] <= q_ids[i])
            def _():
                sums = None
                for h in range(heads):
                    cols = slice(h * HD, (h + 1) * HD)
                    scores = lax.dot_general(
                        qs[i][:rows, cols], ks[j][:rows, cols], (((1,), (1,)), ((), ())),
                        preferred_element_type=jnp.float32,
                    )
                    weights = jnp.exp2(scores).astype(jnp.bfloat16)
                    wide = jnp.concatenate([vs[j][:, cols], ones], axis=1)
                    both = jnp.dot(weights, wide, preferred_element_type=jnp.float32)
                    acc_ref[i, :, cols] += both[:, :HD]
                    sums = both[:, HD:] if h == 0 else jnp.where(lane == h, both[:, HD:], sums)
                acc_ref[i, :, heads * HD :] += sums
    if last:
        for n, i in enumerate((0, 2)):
            keep_ref[n] = acc_ref[i, :, : heads * HD]
            keep_sum[n] = acc_ref[i, :, heads * HD :].T[:8]
        for n, i in enumerate((1, 3)):
            write_share(send_ref.at[n], acc_ref[i, :, : heads * HD], acc_ref[i, :, heads * HD :].T[:8])


def write_share(ref, sums, totals):
    rows = sums.shape[0]
    ref[:rows] = sums.astype(jnp.bfloat16)
    pad = jnp.zeros((8, sums.shape[1] - rows), jnp.float32)
    high = totals.astype(jnp.bfloat16).astype(jnp.float32)
    low = totals - high
    both = jnp.concatenate(
        [jnp.concatenate([high, pad], axis=1), jnp.concatenate([low, pad], axis=1)], axis=0
    )
    ref[rows:] = both.astype(jnp.bfloat16)


def read_totals(ref, rows):
    both = ref[rows:, :rows].astype(jnp.float32)
    return both[:8] + both[8:]


def attend(qs, ks, vs, state, last):
    rows, width = vs[0].shape
    n_keys = len(ks)
    wide = width + HD
    vmem = pl.BlockSpec(memory_space=pltpu.VMEM)
    state_shape = jax.ShapeDtypeStruct((4, rows, wide), jnp.float32)
    if last:
        out_shape = [
            jax.ShapeDtypeStruct((2, rows, width), jnp.float32),
            jax.ShapeDtypeStruct((2, 8, rows), jnp.float32),
            jax.ShapeDtypeStruct((2, rows + ID_ROWS, width), jnp.bfloat16),
        ]
        scratch = [pltpu.VMEM((4, rows, wide), jnp.float32)]
    else:
        out_shape, scratch = [state_shape], []
    first = state is None
    args = [*qs, *ks, *vs] + ([] if first else [state])

    def body(*refs):
        attend_kernel(n_keys, first, last, *refs)

    flops = 4 * n_keys * 3 * rows * rows * HD * 4
    return pl.pallas_call(
        body,
        in_specs=[vmem] * len(args),
        out_specs=[vmem] * len(out_shape),
        out_shape=out_shape,
        scratch_shapes=scratch,
        compiler_params=pltpu.CompilerParams(vmem_limit_bytes=32 * MIB),
        cost_estimate=pl.CostEstimate(
            flops=flops, bytes_accessed=8 * MIB, transcendentals=4 * n_keys * 3 * rows * rows
        ),
        name="attend",
    )(*args)


def fold_kernel(keep_ref, sum_ref, got_ref, own_ref, own_sum, send_ref):
    rows = keep_ref.shape[1]
    own_ref[...] = keep_ref[0] + got_ref[0, :rows].astype(jnp.float32)
    own_sum[...] = sum_ref[0] + read_totals(got_ref.at[0], rows)
    write_share(
        send_ref,
        keep_ref[1] + got_ref[1, :rows].astype(jnp.float32),
        sum_ref[1] + read_totals(got_ref.at[1], rows),
    )


def fold(keep, sums, got):
    _, rows, width = keep.shape
    vmem = pl.BlockSpec(memory_space=pltpu.VMEM)
    return pl.pallas_call(
        fold_kernel,
        in_specs=[vmem] * 3,
        out_specs=[vmem] * 3,
        out_shape=[
            jax.ShapeDtypeStruct((rows, width), jnp.float32),
            jax.ShapeDtypeStruct((8, rows), jnp.float32),
            jax.ShapeDtypeStruct((rows + ID_ROWS, width), jnp.bfloat16),
        ],
        compiler_params=pltpu.CompilerParams(vmem_limit_bytes=8 * MIB),
        name="fold",
    )(keep, sums, got)


def finish_kernel(own_ref, sum_ref, got_ref, out_ref):
    rows, width = out_ref.shape
    total = own_ref[...] + got_ref[:rows].astype(jnp.float32)
    sums = sum_ref[...] + read_totals(got_ref, rows)
    columns = jnp.concatenate([sums, jnp.ones((120, rows), jnp.float32)], axis=0).T
    for h in range(width // HD):
        cols = slice(h * HD, (h + 1) * HD)
        out_ref[:, cols] = (total[:, cols] / columns[:, h : h + 1]).astype(jnp.bfloat16)


def finish(own, sums, got):
    rows, width = own.shape
    vmem = pl.BlockSpec(memory_space=pltpu.VMEM)
    return pl.pallas_call(
        finish_kernel,
        in_specs=[vmem] * 3,
        out_specs=vmem,
        out_shape=jax.ShapeDtypeStruct((rows, width), jnp.bfloat16),
        compiler_params=pltpu.CompilerParams(vmem_limit_bytes=8 * MIB),
        name="finish",
    )(own, sums, got)


def arrange_kernel(slot_ref, here_ref, *refs):
    weights, (out_ref, sems) = refs[:4], refs[4:]
    y_lo, core = here_ref[0], here_ref[1]

    def fetches(r):
        for n, w_ref in enumerate(weights):
            part = (core + n // 2) % 2 * 2 + (y_lo + n % 2) % 2
            yield pltpu.make_async_copy(w_ref.at[slot_ref[r]], out_ref.at[r, part], sems.at[r, n])

    for r in range(8):
        for copy in fetches(r):
            copy.start()
    for r in range(8):
        for copy in fetches(r):
            copy.wait()


def arrange_weight(weights, slots, here):
    _, cols, width = weights[0].shape
    anywhere = pl.BlockSpec(memory_space=pl.ANY)
    return pl.pallas_call(
        arrange_kernel,
        in_specs=[pl.BlockSpec(memory_space=pltpu.SMEM)] * 2 + [anywhere] * 4,
        out_specs=pl.BlockSpec(memory_space=pltpu.VMEM),
        out_shape=jax.ShapeDtypeStruct((8, 4, cols, width), weights[0].dtype),
        scratch_shapes=[pltpu.SemaphoreType.DMA((8, 4))],
        compiler_params=pltpu.CompilerParams(vmem_limit_bytes=16 * MIB),
        cost_estimate=pl.CostEstimate(flops=0, bytes_accessed=8 * MIB, transcendentals=0),
        name="arrange",
    )(slots, here, *weights)


def project_kernel(n, low, *refs):
    blocks, (w_ref, out_ref) = refs[:n], refs[-2:]
    width = blocks[0].shape[1]
    total = refs[n][...] if low else None
    for r in range(n):
        term = lax.dot_general(
            blocks[r][...], w_ref[low + r].reshape(-1, width), (((1,), (1,)), ((), ())),
            preferred_element_type=jnp.float32,
        )
        total = term if total is None else total + term
    out_ref[...] = total.astype(out_ref.dtype)


def project_part(blocks, low, weight, acc):
    n = len(blocks)
    rows, width = blocks[0].shape
    columns = weight.shape[1] * weight.shape[2]
    vmem = pl.BlockSpec(memory_space=pltpu.VMEM)
    args = [*blocks] + ([acc] if low else []) + [weight]

    def body(*refs):
        project_kernel(n, low, *refs)

    return pl.pallas_call(
        body,
        in_specs=[vmem] * len(args),
        out_specs=vmem,
        out_shape=jax.ShapeDtypeStruct((rows, columns), jnp.bfloat16 if low + n == 8 else jnp.float32),
        compiler_params=pltpu.CompilerParams(vmem_limit_bytes=16 * MIB),
        cost_estimate=pl.CostEstimate(
            flops=2 * rows * n * width * columns, bytes_accessed=n * width * columns * 2, transcendentals=0
        ),
        name="project",
    )(*args)


RING_SLOT = (0, 2, 7, 6, 4, 3, 5, 1)


def regroup_weight(out_weight):
    pairs = []
    for c in range(N_CTX):
        c_lo, c_z, c_core = c // 16, (c // 2) % N_Z, c % 2
        for t in range(N_TP):
            pairs.append(((4 * t + c_core * 2 + c_lo) * N_TP + c_z, c * N_TP + t))
    return lax.ppermute(out_weight.T, ("ctx", "tp"), pairs)


def on_device(tokens, qkv_weight, query_gain, key_gain, out_weight, block_ids):
    places = sender_places()
    c = lax.axis_index("ctx")
    here = jnp.stack([c // 16, c % 2]).astype(jnp.int32)
    distance = (places - (c // 2) % N_Z + N_Z) % N_Z
    slots = sum(jnp.where(distance == d, slot, 0) for d, slot in enumerate(RING_SLOT))

    blocks, out_ring = gather_tp_and_ring(tokens, regroup_weight(out_weight))
    weight = order_weight(qkv_weight.transpose(1, 0, 2), places)
    (partial,) = qkv_part(blocks[:4], 0, weight, None)
    (partial,) = qkv_part(blocks[4:6], 4, weight, partial)
    q_flat, k_flat, values, squares = qkv_part(blocks[6:], 6, weight, partial)

    v_up, v_down = [values, move(values, z=1)], [values, move(values, z=-1)]
    pair_sum = squares + move(squares, y_hi=1)
    parts = [pair_sum] + [move(pair_sum, x=x) for x in (2, 1, 3)]
    queries, keys = norm(
        block_ids[:1], parts, after(q_flat, v_up[1], v_down[1], *out_ring[1:]), k_flat, query_gain.reshape(1, -1), key_gain.reshape(1, -1)
    )

    mate = move(queries, core=1)
    across = move(queries, y_lo=1)
    qs = [queries, mate, across, move(across, core=1)]

    k_up, k_down = [keys, move(keys, z=1)], [keys, move(keys, z=-1)]
    rings = ((v_up, 1), (v_down, -1), (k_up, 1), (k_down, -1))
    for ring, z in rings:
        ring.append(move(ring[1], z=z))
    (state,) = attend(qs, [keys, k_up[1], k_down[1]], [values, v_up[1], v_down[1]], None, False)
    for ring, z in rings:
        ring.append(move(after(ring[2], state), z=z))
    (state,) = attend(qs, [k_up[2], k_down[2]], [v_up[2], v_down[2]], state, False)
    k_far = move(after(k_up[3], state), z=1)
    v_far = move(after(v_down[3], state), z=-1)
    (state,) = attend(qs, [k_up[3], k_down[3]], [v_up[3], v_down[3]], state, False)
    keep, sums, send = attend(qs, [k_far], [v_far], state, True)

    out_own = jnp.concatenate(out_ring)
    out_far = move(after(out_own, across), y_lo=1)
    out_mate, out_mate_far = move(after(out_own, state), core=1), move(after(out_far, state), core=1)
    out_whole = arrange_weight([out_own, out_far, out_mate, out_mate_far], slots, here)

    own, sums, send = fold(keep, sums, move(send, core=1))
    attention = finish(own, sums, move(send, y_lo=1))
    blocks = gather_tp(attention)
    total = project_part(blocks[:6], 0, out_whole, None)
    return project_part(blocks[6:], 6, out_whole, total)


def solution(mesh):
    in_specs = (P("ctx", "tp"), P(None, None, "tp"), P("tp"), P("tp"), P("tp", "ctx"), P("ctx"))
    out_specs = P("ctx", "tp")
    return jax.shard_map(
        on_device, mesh=mesh, in_specs=in_specs, out_specs=out_specs, check_vma=False
    )
```

```python
import math

import jax
import jax.numpy as jnp
from jax import lax
from jax.experimental import pallas as pl
from jax.experimental.pallas import tpu as pltpu
from jax.sharding import PartitionSpec as P

HEADS = 24
HD = 128
ID_ROWS = 16
N_Z = 8
N_X = 4
N_TP = 8
N_CTX = 32
MIB = 1 << 20


def move(value, x=0, y_hi=0, y_lo=0, z=0, core=0):
    pairs = []
    for c in range(N_CTX):
        for t in range(N_TP):
            c_lo, c_z, c_core = c // 16, (c // 2) % 8, c % 2
            t_x, t_hi = t // 2, t % 2
            dst_c = ((c_lo + y_lo) % 2) * 16 + ((c_z + z) % N_Z) * 2 + (c_core + core) % 2
            dst_t = ((t_x + x) % N_X) * 2 + (t_hi + y_hi) % 2
            pairs.append((c * N_TP + t, dst_c * N_TP + dst_t))
    return lax.ppermute(value, ("ctx", "tp"), pairs)


TP_STEPS = [(0, 0), (0, 1), (1, 0), (3, 0), (1, 1), (3, 1), (2, 0), (2, 1)]


def after(value, *others):
    return lax.optimization_barrier((value, *others))[0]


def gather_tp(upper, lower):
    both = jnp.concatenate([upper, move(upper, y_hi=1)])
    along = jnp.concatenate([lower] + [move(lower, x=x) for x in (1, 3, 2)])
    far = move(along, y_hi=1)
    return [both] + [move(both, x=x) for x in (1, 3, 2)], along, far


def gather_blocks(value):
    blocks = [value]
    for r in range(1, 8):
        ties = {4: (1, 3), 5: (2, 3), 6: (4,), 7: (5,)}.get(r)
        source = after(value, *[blocks[b] for b in ties]) if ties else value
        blocks.append(move(source, x=TP_STEPS[r][0], y_hi=TP_STEPS[r][1]))
    return blocks


def sender_places():
    t = lax.axis_index("tp")
    t_x, t_hi = t // 2, t % 2
    return jnp.stack(
        [((t_x - x + N_X) % N_X) * 2 + (t_hi - y_hi + 2) % 2 for x, y_hi in TP_STEPS]
    ).astype(jnp.int32)


def order_kernel(place_ref, w_ref, out_ref, sems):
    feats = out_ref.shape[1] // 8

    def fetch(r):
        start = pl.multiple_of(place_ref[r] * feats, feats)
        return pltpu.make_async_copy(
            w_ref.at[:, pl.ds(start, feats), :], out_ref.at[:, pl.ds(r * feats, feats), :], sems.at[r]
        )

    for r in range(8):
        fetch(r).start()
    for r in range(8):
        fetch(r).wait()


def order_weight(weight, places):
    return pl.pallas_call(
        order_kernel,
        in_specs=[pl.BlockSpec(memory_space=pltpu.SMEM), pl.BlockSpec(memory_space=pl.ANY)],
        out_specs=pl.BlockSpec(memory_space=pltpu.VMEM),
        out_shape=jax.ShapeDtypeStruct(weight.shape, weight.dtype),
        scratch_shapes=[pltpu.SemaphoreType.DMA((8,))],
        compiler_params=pltpu.CompilerParams(vmem_limit_bytes=32 * MIB),
        cost_estimate=pl.CostEstimate(flops=0, bytes_accessed=24 * MIB, transcendentals=0),
        name="order",
    )(places, weight)


def qkv_kernel(n, low, first, last, *refs):
    toks, refs = refs[:n], refs[n:]
    acc_in, refs = (None, refs) if first else (refs[0], refs[1:])
    w_ref, outs = refs[0], refs[1:]
    if last:
        out_w, outs = outs[0], outs[1:]
    feats = toks[0].shape[1]
    wide = jnp.concatenate([tok[...] for tok in toks], axis=1)
    sums = []
    for p in range(3):
        rows = slice(low * feats, (low + n) * feats)
        term = jnp.dot(wide, w_ref[p, rows, :], preferred_element_type=jnp.float32)
        if not first:
            term = acc_in[p] + term
        if not last:
            outs[0][p] = term
        sums.append(term)
    if not last:
        return
    q, k, v = sums
    q_ref, k_ref, v_ref, sq_ref = outs
    q_ref[...] = q
    k_ref[...] = k
    v_ref[: v.shape[0]] = v.astype(jnp.bfloat16)
    v_ref[v.shape[0] :] = out_w[...]
    q_sq = jnp.sum(q * q, axis=1, keepdims=True)
    k_sq = jnp.sum(k * k, axis=1, keepdims=True)
    lane = lax.broadcasted_iota(jnp.int32, (q.shape[0], 128), 1)
    both = jnp.where(lane == 0, q_sq, jnp.where(lane == 1, k_sq, 0.0))
    sq_ref[...] = both.T[:8]


def qkv_part(blocks, low, weight, acc, out_block=None):
    n = len(blocks)
    rows, feats = blocks[0].shape
    width = weight.shape[2]
    first, last = acc is None, low + n == 8
    vmem = pl.BlockSpec(memory_space=pltpu.VMEM)
    args = [*blocks] + ([] if first else [acc]) + [weight]
    if last:
        args.append(out_block)
        out_shape = [
            jax.ShapeDtypeStruct((rows, width), jnp.float32),
            jax.ShapeDtypeStruct((rows, width), jnp.float32),
            jax.ShapeDtypeStruct((rows + out_block.shape[0], width), jnp.bfloat16),
            jax.ShapeDtypeStruct((8, rows), jnp.float32),
        ]
    else:
        out_shape = [jax.ShapeDtypeStruct((3, rows, width), jnp.float32)]

    def body(*refs):
        qkv_kernel(n, low, first, last, *refs)

    return pl.pallas_call(
        body,
        in_specs=[vmem] * len(args),
        out_specs=[vmem] * len(out_shape),
        out_shape=out_shape,
        compiler_params=pltpu.CompilerParams(vmem_limit_bytes=32 * MIB),
        cost_estimate=pl.CostEstimate(
            flops=2 * rows * n * feats * 3 * width, bytes_accessed=n * feats * 3 * width * 2, transcendentals=0
        ),
        name="qkv",
    )(*args)


def norm_kernel(id_ref, s0, s1, s2, s3, q_ref, k_ref, qg_ref, kg_ref, q_out, k_out):
    rows = q_ref.shape[0]
    total = s0[...] + s1[...] + s2[...] + s3[...]
    inverse = lax.rsqrt(total * (1.0 / (HEADS * HD)) + 1e-06)
    columns = jnp.concatenate([inverse, jnp.zeros((120, rows), jnp.float32)], axis=0).T
    q_scale = math.log2(math.e) / math.sqrt(HD)
    q_out[:rows] = (q_ref[...] * columns[:, 0:1] * (qg_ref[...] * q_scale)).astype(jnp.bfloat16)
    k_out[:rows] = (k_ref[...] * columns[:, 1:2] * kg_ref[...]).astype(jnp.bfloat16)
    span = jnp.full((ID_ROWS, q_ref.shape[1]), id_ref[0].astype(jnp.float32), jnp.float32)
    q_out[rows:] = span.astype(jnp.bfloat16)
    k_out[rows:] = span.astype(jnp.bfloat16)


def norm(span_id, squares, q, k, q_gain, k_gain):
    rows, width = q.shape
    vmem = pl.BlockSpec(memory_space=pltpu.VMEM)
    out = jax.ShapeDtypeStruct((rows + ID_ROWS, width), jnp.bfloat16)
    return pl.pallas_call(
        norm_kernel,
        in_specs=[pl.BlockSpec(memory_space=pltpu.SMEM)] + [vmem] * 8,
        out_specs=[vmem] * 2,
        out_shape=[out, out],
        compiler_params=pltpu.CompilerParams(vmem_limit_bytes=12 * MIB),
        name="norm",
    )(span_id, *squares, q, k, q_gain, k_gain)


def attend_kernel(n_keys, first, last, *refs):
    qs, ks, vs = refs[:4], refs[4 : 4 + n_keys], refs[4 + n_keys : 4 + 2 * n_keys]
    rest = refs[4 + 2 * n_keys :]
    rows = qs[0].shape[0] - ID_ROWS
    heads = vs[0].shape[1] // HD
    if first:
        acc_ref, = rest[:1]
        acc_ref[...] = jnp.zeros_like(acc_ref)
    elif last:
        acc_in, keep_ref, keep_sum, send_ref, acc_ref = rest
        acc_ref[...] = acc_in[...]
    else:
        acc_in, acc_ref = rest
        acc_ref[...] = acc_in[...]
    lane = lax.broadcasted_iota(jnp.int32, (rows, HD), 1)
    ones = jnp.ones((rows, HD), jnp.bfloat16)
    q_ids = [jnp.max(q[rows:, :HD].astype(jnp.float32)) for q in qs]
    k_ids = [jnp.max(k[rows:, :HD].astype(jnp.float32)) for k in ks]
    for i in range(4):
        for j in range(n_keys):

            @pl.when(k_ids[j] <= q_ids[i])
            def _():
                sums = None
                for h in range(heads):
                    cols = slice(h * HD, (h + 1) * HD)
                    scores = lax.dot_general(
                        qs[i][:rows, cols], ks[j][:rows, cols], (((1,), (1,)), ((), ())),
                        preferred_element_type=jnp.float32,
                    )
                    weights = jnp.exp2(scores).astype(jnp.bfloat16)
                    wide = jnp.concatenate([vs[j][:rows, cols], ones], axis=1)
                    both = jnp.dot(weights, wide, preferred_element_type=jnp.float32)
                    acc_ref[i, :, cols] += both[:, :HD]
                    sums = both[:, HD:] if h == 0 else jnp.where(lane == h, both[:, HD:], sums)
                acc_ref[i, :, heads * HD :] += sums
    if last:
        for n, i in enumerate((0, 2)):
            keep_ref[n] = acc_ref[i, :, : heads * HD]
            keep_sum[n] = acc_ref[i, :, heads * HD :].T[:8]
        for n, i in enumerate((1, 3)):
            write_share(send_ref.at[n], acc_ref[i, :, : heads * HD], acc_ref[i, :, heads * HD :].T[:8])


def write_share(ref, sums, totals):
    rows = sums.shape[0]
    ref[:rows] = sums.astype(jnp.bfloat16)
    pad = jnp.zeros((8, sums.shape[1] - rows), jnp.float32)
    high = totals.astype(jnp.bfloat16).astype(jnp.float32)
    low = totals - high
    both = jnp.concatenate(
        [jnp.concatenate([high, pad], axis=1), jnp.concatenate([low, pad], axis=1)], axis=0
    )
    ref[rows:] = both.astype(jnp.bfloat16)


def read_totals(ref, rows):
    both = ref[rows:, :rows].astype(jnp.float32)
    return both[:8] + both[8:]


def attend(qs, ks, vs, state, last):
    rows, width = qs[0].shape[0] - ID_ROWS, vs[0].shape[1]
    n_keys = len(ks)
    wide = width + HD
    vmem = pl.BlockSpec(memory_space=pltpu.VMEM)
    state_shape = jax.ShapeDtypeStruct((4, rows, wide), jnp.float32)
    if last:
        out_shape = [
            jax.ShapeDtypeStruct((2, rows, width), jnp.float32),
            jax.ShapeDtypeStruct((2, 8, rows), jnp.float32),
            jax.ShapeDtypeStruct((2, rows + ID_ROWS, width), jnp.bfloat16),
        ]
        scratch = [pltpu.VMEM((4, rows, wide), jnp.float32)]
    else:
        out_shape, scratch = [state_shape], []
    first = state is None
    args = [*qs, *ks, *vs] + ([] if first else [state])

    def body(*refs):
        attend_kernel(n_keys, first, last, *refs)

    flops = 4 * n_keys * 3 * rows * rows * HD * 4
    return pl.pallas_call(
        body,
        in_specs=[vmem] * len(args),
        out_specs=[vmem] * len(out_shape),
        out_shape=out_shape,
        scratch_shapes=scratch,
        compiler_params=pltpu.CompilerParams(vmem_limit_bytes=32 * MIB),
        cost_estimate=pl.CostEstimate(
            flops=flops, bytes_accessed=8 * MIB, transcendentals=4 * n_keys * 3 * rows * rows
        ),
        name="attend",
    )(*args)


def fold_kernel(keep_ref, sum_ref, got_ref, own_ref, own_sum, send_ref):
    rows = keep_ref.shape[1]
    own_ref[...] = keep_ref[0] + got_ref[0, :rows].astype(jnp.float32)
    own_sum[...] = sum_ref[0] + read_totals(got_ref.at[0], rows)
    write_share(
        send_ref,
        keep_ref[1] + got_ref[1, :rows].astype(jnp.float32),
        sum_ref[1] + read_totals(got_ref.at[1], rows),
    )


def fold(keep, sums, got):
    _, rows, width = keep.shape
    vmem = pl.BlockSpec(memory_space=pltpu.VMEM)
    return pl.pallas_call(
        fold_kernel,
        in_specs=[vmem] * 3,
        out_specs=[vmem] * 3,
        out_shape=[
            jax.ShapeDtypeStruct((rows, width), jnp.float32),
            jax.ShapeDtypeStruct((8, rows), jnp.float32),
            jax.ShapeDtypeStruct((rows + ID_ROWS, width), jnp.bfloat16),
        ],
        compiler_params=pltpu.CompilerParams(vmem_limit_bytes=8 * MIB),
        name="fold",
    )(keep, sums, got)


def finish_kernel(own_ref, sum_ref, got_ref, upper_ref, lower_ref):
    half, width = upper_ref.shape
    rows = 2 * half
    total = own_ref[...] + got_ref[:rows].astype(jnp.float32)
    sums = sum_ref[...] + read_totals(got_ref, rows)
    columns = jnp.concatenate([sums, jnp.ones((120, rows), jnp.float32)], axis=0).T
    for h in range(width // HD):
        cols = slice(h * HD, (h + 1) * HD)
        normed = (total[:, cols] / columns[:, h : h + 1]).astype(jnp.bfloat16)
        upper_ref[:, cols] = normed[:half]
        lower_ref[:, cols] = normed[half:]


def finish(own, sums, got):
    rows, width = own.shape
    vmem = pl.BlockSpec(memory_space=pltpu.VMEM)
    half = jax.ShapeDtypeStruct((rows // 2, width), jnp.bfloat16)
    return pl.pallas_call(
        finish_kernel,
        in_specs=[vmem] * 3,
        out_specs=[vmem] * 2,
        out_shape=[half, half],
        compiler_params=pltpu.CompilerParams(vmem_limit_bytes=8 * MIB),
        name="finish",
    )(own, sums, got)


def arrange_kernel(spot_ref, here_ref, own_ref, mate_ref, out_ref):
    y_lo, core = here_ref[0], here_ref[1]
    for n in range(4):
        held, far = (own_ref, mate_ref)[n // 2], n % 2
        part = lax.rem(core + n // 2, 2) * 2 + lax.rem(y_lo + far, 2)
        for s in range(8):
            out_ref[spot_ref[s], part] = held[far * 8 + s]


def arrange_weight(own, mate, spots, here):
    _, cols, width = own.shape
    vmem = pl.BlockSpec(memory_space=pltpu.VMEM)
    return pl.pallas_call(
        arrange_kernel,
        in_specs=[pl.BlockSpec(memory_space=pltpu.SMEM)] * 2 + [vmem] * 2,
        out_specs=vmem,
        out_shape=jax.ShapeDtypeStruct((8, 4, cols, width), own.dtype),
        compiler_params=pltpu.CompilerParams(vmem_limit_bytes=16 * MIB),
        cost_estimate=pl.CostEstimate(flops=0, bytes_accessed=8 * MIB, transcendentals=0),
        name="arrange",
    )(spots, here, own, mate)


HERE, THERE = (0, 2, 3, 6), (1, 4, 5, 7)


def term_of(rows, w_ref, r):
    weight = w_ref[r].reshape(-1, rows.shape[1])
    return lax.dot_general(rows, weight, (((1,), (1,)), ((), ())), preferred_element_type=jnp.float32)


def project_kernel(b0, b1, b2, b3, along, w_ref, upper_ref, lower_ref):
    half = upper_ref.shape[0]
    upper = lower = None
    for n, both in enumerate((b0, b1, b2, b3)):
        for rows, r in ((both[:half], HERE[n]), (both[half:], THERE[n])):
            term = term_of(rows, w_ref, r)
            upper = term if upper is None else upper + term
        term = term_of(along[n * half : (n + 1) * half], w_ref, HERE[n])
        lower = term if lower is None else lower + term
    upper_ref[...] = upper.astype(jnp.bfloat16)
    lower_ref[...] = lower


def project_last_kernel(upper_ref, lower_ref, far, w_ref, out_ref):
    half = upper_ref.shape[0]
    out_ref[:half] = upper_ref[...]
    lower = lower_ref[...]
    for n in range(4):
        lower = lower + term_of(far[n * half : (n + 1) * half], w_ref, THERE[n])
    out_ref[half:] = lower.astype(jnp.bfloat16)


def project(both, along, far, weight):
    rows, width = both[0].shape
    half = rows // 2
    columns = weight.shape[1] * weight.shape[2]
    vmem = pl.BlockSpec(memory_space=pltpu.VMEM)

    def call(kernel, args, out_shape, terms):
        return pl.pallas_call(
            kernel,
            in_specs=[vmem] * len(args),
            out_specs=[vmem] * len(out_shape),
            out_shape=out_shape,
            compiler_params=pltpu.CompilerParams(vmem_limit_bytes=16 * MIB),
            cost_estimate=pl.CostEstimate(
                flops=2 * half * terms * width * columns, bytes_accessed=8 * width * columns * 2, transcendentals=0
            ),
            name="project",
        )(*args)

    upper, lower = call(
        project_kernel,
        [*both, along, weight],
        [
            jax.ShapeDtypeStruct((half, columns), jnp.bfloat16),
            jax.ShapeDtypeStruct((half, columns), jnp.float32),
        ],
        12,
    )
    return call(
        project_last_kernel,
        [upper, lower, far, weight],
        [jax.ShapeDtypeStruct((rows, columns), jnp.bfloat16)],
        4,
    )[0]


RING_SLOT = (0, 2, 4, 6, 7, 5, 3, 1)


def regroup_weight(out_weight):
    pairs = []
    for c in range(N_CTX):
        c_lo, c_z, c_core = c // 16, (c // 2) % N_Z, c % 2
        for t in range(N_TP):
            pairs.append(((4 * t + c_core * 2 + c_lo) * N_TP + c_z, c * N_TP + t))
    return lax.ppermute(out_weight.T, ("ctx", "tp"), pairs)


def on_device(tokens, qkv_weight, query_gain, key_gain, out_weight, block_ids):
    places = sender_places()
    c = lax.axis_index("ctx")
    here = jnp.stack([c // 16, c % 2]).astype(jnp.int32)
    distance = (places - (c // 2) % N_Z + N_Z) % N_Z
    slots = sum(jnp.where(distance == d, slot, 0) for d, slot in enumerate(RING_SLOT))
    step = jnp.arange(8, dtype=jnp.int32)
    spots = jnp.sum(jnp.where(slots[None, :] == step[:, None], step[None, :], 0), axis=1).astype(jnp.int32)

    blocks = gather_blocks(tokens)
    out_block = regroup_weight(out_weight)
    weight = order_weight(qkv_weight.transpose(1, 0, 2), places)
    (partial,) = qkv_part(blocks[:4], 0, weight, None)
    (partial,) = qkv_part(blocks[4:6], 4, weight, partial)
    q_flat, k_flat, values, squares = qkv_part(blocks[6:], 6, weight, partial, out_block)

    v_up, v_down = [values, move(values, z=1)], [values, move(values, z=-1)]
    pair_sum = squares + move(squares, y_hi=1)
    parts = [pair_sum] + [move(pair_sum, x=x) for x in (2, 1, 3)]
    queries, keys = norm(
        block_ids[:1], parts, after(q_flat, v_up[1], v_down[1]), k_flat, query_gain.reshape(1, -1), key_gain.reshape(1, -1)
    )

    mate = move(queries, core=1)
    across = move(queries, y_lo=1)
    qs = [queries, mate, across, move(across, core=1)]

    rows = block_ids.shape[0]
    for _ in range(2):
        v_up.append(move(v_up[-1], z=1))
        v_down.append(move(v_down[-1], z=-1))
    v_far = move(v_down[3], z=-1)
    early = jnp.stack([v[rows:] for v in (values, v_up[1], v_down[1], v_up[2], v_down[2])])
    late = jnp.stack([v[rows:] for v in (v_up[3], v_down[3], v_far)])
    early_far, late_far = move(after(early, across), y_lo=1), move(late, y_lo=1)

    k_up, k_down = [keys, move(keys, z=1)], [keys, move(keys, z=-1)]
    k_up.append(move(k_up[1], z=1))
    k_down.append(move(k_down[1], z=-1))
    (state,) = attend(qs, [keys, k_up[1], k_down[1]], [values, v_up[1], v_down[1]], None, False)
    k_up.append(move(after(k_up[2], state), z=1))
    k_down.append(move(after(k_down[2], state), z=-1))
    (state,) = attend(qs, [k_up[2], k_down[2]], [v_up[2], v_down[2]], state, False)
    k_far = move(after(k_up[3], state), z=1)
    (state,) = attend(qs, [k_up[3], k_down[3]], [v_up[3], v_down[3]], state, False)
    keep, sums, send = attend(qs, [k_far], [v_far], state, True)

    own, sums, send = fold(keep, sums, move(send, core=1))
    out_own = jnp.concatenate([early, late, early_far, after(late_far, own)])
    out_mate = move(out_own, core=1)
    upper, lower = finish(own, sums, move(send, y_lo=1))
    both, along, far = gather_tp(upper, lower)
    out_whole = arrange_weight(out_own, out_mate, spots, here)
    return project(both, along, far, out_whole)


def solution(mesh):
    in_specs = (P("ctx", "tp"), P(None, None, "tp"), P("tp"), P("tp"), P("tp", "ctx"), P("ctx"))
    out_specs = P("ctx", "tp")
    return jax.shard_map(
        on_device, mesh=mesh, in_specs=in_specs, out_specs=out_specs, check_vma=False
    )
```

```python
import math

import jax
import jax.numpy as jnp
from jax import lax
from jax.experimental import pallas as pl
from jax.experimental.pallas import tpu as pltpu
from jax.sharding import PartitionSpec as P

HEADS = 24
HD = 128
ID_ROWS = 16
N_Z = 8
N_X = 4
N_TP = 8
N_CTX = 32
MIB = 1 << 20


def move(value, x=0, y_hi=0, y_lo=0, z=0, core=0):
    pairs = []
    for c in range(N_CTX):
        for t in range(N_TP):
            c_lo, c_z, c_core = c // 16, (c // 2) % 8, c % 2
            t_x, t_hi = t // 2, t % 2
            dst_c = ((c_lo + y_lo) % 2) * 16 + ((c_z + z) % N_Z) * 2 + (c_core + core) % 2
            dst_t = ((t_x + x) % N_X) * 2 + (t_hi + y_hi) % 2
            pairs.append((c * N_TP + t, dst_c * N_TP + dst_t))
    return lax.ppermute(value, ("ctx", "tp"), pairs)


TP_STEPS = [(0, 0), (1, 0), (3, 0), (2, 0), (0, 1), (1, 1), (3, 1), (2, 1)]


def after(value, *others):
    return lax.optimization_barrier((value, *others))[0]


def gather_tp(upper, lower):
    both = jnp.concatenate([upper, move(upper, y_hi=1)])
    along = jnp.concatenate([lower] + [move(lower, x=x) for x in (1, 3, 2)])
    far = move(along, y_hi=1)
    return [both] + [move(both, x=x) for x in (1, 3, 2)], along, far


def sender_places():
    t = lax.axis_index("tp")
    t_x, t_hi = t // 2, t % 2
    return jnp.stack(
        [((t_x - x + N_X) % N_X) * 2 + (t_hi - y_hi + 2) % 2 for x, y_hi in TP_STEPS]
    ).astype(jnp.int32)


def order_kernel(place_ref, w_ref, out_ref, sems):
    feats = out_ref.shape[1] // 8

    def fetch(r):
        start = pl.multiple_of(place_ref[r] * feats, feats)
        return pltpu.make_async_copy(
            w_ref.at[:, pl.ds(start, feats), :], out_ref.at[:, pl.ds(r * feats, feats), :], sems.at[r]
        )

    for r in range(8):
        fetch(r).start()
    for r in range(8):
        fetch(r).wait()


def order_weight(weight, places):
    return pl.pallas_call(
        order_kernel,
        in_specs=[pl.BlockSpec(memory_space=pltpu.SMEM), pl.BlockSpec(memory_space=pl.ANY)],
        out_specs=pl.BlockSpec(memory_space=pltpu.VMEM),
        out_shape=jax.ShapeDtypeStruct(weight.shape, weight.dtype),
        scratch_shapes=[pltpu.SemaphoreType.DMA((8,))],
        compiler_params=pltpu.CompilerParams(vmem_limit_bytes=32 * MIB),
        cost_estimate=pl.CostEstimate(flops=0, bytes_accessed=24 * MIB, transcendentals=0),
        name="order",
    )(places, weight)


def product(rows, w_ref, p, block):
    wide = jnp.concatenate(rows, axis=1) if len(rows) > 1 else rows[0]
    feats = w_ref.shape[1] // 8
    return jnp.dot(
        wide, w_ref[p, block * feats : block * feats + wide.shape[1], :], preferred_element_type=jnp.float32
    )


def lower_kernel(block, *refs):
    held, w_ref, out_ref = refs[0], refs[-2], refs[-1]
    half = held.shape[0] // 4
    rows = [held[n * half : (n + 1) * half] for n in range(4)]
    for p in range(3):
        term = product(rows, w_ref, p, block)
        out_ref[p] = term if block == 0 else refs[1][p] + term


def upper_kernel(b0, b1, b2, w_ref, out_ref):
    half = b0.shape[0] // 2
    for p in range(3):
        here = product([b[:half] for b in (b0, b1, b2)], w_ref, p, 0)
        out_ref[p] = here + product([b[half:] for b in (b0, b1, b2)], w_ref, p, 4)


def last_kernel(b3, upper_ref, lower_ref, w_ref, out_w, q_ref, k_ref, v_ref, sq_ref):
    half = b3.shape[0] // 2

    def whole(p):
        upper = upper_ref[p] + product([b3[:half]], w_ref, p, 3) + product([b3[half:]], w_ref, p, 7)
        return jnp.concatenate([upper, lower_ref[p]], axis=0)

    q, k, v = [whole(p) for p in range(3)]
    q_ref[...] = q
    k_ref[...] = k
    v_ref[: v.shape[0]] = v.astype(jnp.bfloat16)
    v_ref[v.shape[0] :] = out_w[...]
    q_sq = jnp.sum(q * q, axis=1, keepdims=True)
    k_sq = jnp.sum(k * k, axis=1, keepdims=True)
    lane = lax.broadcasted_iota(jnp.int32, (q.shape[0], 128), 1)
    both = jnp.where(lane == 0, q_sq, jnp.where(lane == 1, k_sq, 0.0))
    sq_ref[...] = both.T[:8]


def qkv(firsts, along, far, weight, out_block):
    rows, feats = firsts[0].shape
    half = rows // 2
    width = weight.shape[2]
    vmem = pl.BlockSpec(memory_space=pltpu.VMEM)
    share = jax.ShapeDtypeStruct((3, half, width), jnp.float32)

    def call(kernel, args, out_shape, blocks):
        return pl.pallas_call(
            kernel,
            in_specs=[vmem] * len(args),
            out_specs=[vmem] * len(out_shape),
            out_shape=out_shape,
            compiler_params=pltpu.CompilerParams(vmem_limit_bytes=32 * MIB),
            cost_estimate=pl.CostEstimate(
                flops=2 * half * blocks * feats * 3 * width,
                bytes_accessed=blocks * feats * 3 * width * 2,
                transcendentals=0,
            ),
            name="qkv",
        )(*args)

    def lower_part(block, *args):
        return call(lambda *refs: lower_kernel(block, *refs), [*args, weight], [share], 4)[0]

    lower = lower_part(0, along)
    lower = lower_part(4, far, lower)
    (upper,) = call(upper_kernel, [*firsts[:3], weight], [share], 6)
    whole = jax.ShapeDtypeStruct((rows, width), jnp.float32)
    return call(
        last_kernel,
        [firsts[3], upper, lower, weight, out_block],
        [
            whole,
            whole,
            jax.ShapeDtypeStruct((rows + out_block.shape[0], width), jnp.bfloat16),
            jax.ShapeDtypeStruct((8, rows), jnp.float32),
        ],
        2,
    )


def norm_kernel(id_ref, s0, s1, s2, s3, q_ref, k_ref, qg_ref, kg_ref, q_out, k_out):
    rows = q_ref.shape[0]
    total = s0[...] + s1[...] + s2[...] + s3[...]
    inverse = lax.rsqrt(total * (1.0 / (HEADS * HD)) + 1e-06)
    columns = jnp.concatenate([inverse, jnp.zeros((120, rows), jnp.float32)], axis=0).T
    q_scale = math.log2(math.e) / math.sqrt(HD)
    q_out[:rows] = (q_ref[...] * columns[:, 0:1] * (qg_ref[...] * q_scale)).astype(jnp.bfloat16)
    k_out[:rows] = (k_ref[...] * columns[:, 1:2] * kg_ref[...]).astype(jnp.bfloat16)
    span = jnp.full((ID_ROWS, q_ref.shape[1]), id_ref[0].astype(jnp.float32), jnp.float32)
    q_out[rows:] = span.astype(jnp.bfloat16)
    k_out[rows:] = span.astype(jnp.bfloat16)


def norm(span_id, squares, q, k, q_gain, k_gain):
    rows, width = q.shape
    vmem = pl.BlockSpec(memory_space=pltpu.VMEM)
    out = jax.ShapeDtypeStruct((rows + ID_ROWS, width), jnp.bfloat16)
    return pl.pallas_call(
        norm_kernel,
        in_specs=[pl.BlockSpec(memory_space=pltpu.SMEM)] + [vmem] * 8,
        out_specs=[vmem] * 2,
        out_shape=[out, out],
        compiler_params=pltpu.CompilerParams(vmem_limit_bytes=12 * MIB),
        name="norm",
    )(span_id, *squares, q, k, q_gain, k_gain)


def attend_kernel(n_keys, first, last, *refs):
    qs, ks, vs = refs[:4], refs[4 : 4 + n_keys], refs[4 + n_keys : 4 + 2 * n_keys]
    rest = refs[4 + 2 * n_keys :]
    rows = qs[0].shape[0] - ID_ROWS
    heads = vs[0].shape[1] // HD
    if first:
        acc_ref, = rest[:1]
        acc_ref[...] = jnp.zeros_like(acc_ref)
    elif last:
        acc_in, keep_ref, keep_sum, send_ref, acc_ref = rest
        acc_ref[...] = acc_in[...]
    else:
        acc_in, acc_ref = rest
        acc_ref[...] = acc_in[...]
    lane = lax.broadcasted_iota(jnp.int32, (rows, HD), 1)
    ones = jnp.ones((rows, HD), jnp.bfloat16)
    q_ids = [jnp.max(q[rows:, :HD].astype(jnp.float32)) for q in qs]
    k_ids = [jnp.max(k[rows:, :HD].astype(jnp.float32)) for k in ks]
    for i in range(4):
        for j in range(n_keys):

            @pl.when(k_ids[j] <= q_ids[i])
            def _():
                sums = None
                for h in range(heads):
                    cols = slice(h * HD, (h + 1) * HD)
                    scores = lax.dot_general(
                        qs[i][:rows, cols], ks[j][:rows, cols], (((1,), (1,)), ((), ())),
                        preferred_element_type=jnp.float32,
                    )
                    weights = jnp.exp2(scores).astype(jnp.bfloat16)
                    wide = jnp.concatenate([vs[j][:rows, cols], ones], axis=1)
                    both = jnp.dot(weights, wide, preferred_element_type=jnp.float32)
                    acc_ref[i, :, cols] += both[:, :HD]
                    sums = both[:, HD:] if h == 0 else jnp.where(lane == h, both[:, HD:], sums)
                acc_ref[i, :, heads * HD :] += sums
    if last:
        for n, i in enumerate((0, 2)):
            keep_ref[n] = acc_ref[i, :, : heads * HD]
            keep_sum[n] = acc_ref[i, :, heads * HD :].T[:8]
        for n, i in enumerate((1, 3)):
            write_share(send_ref.at[n], acc_ref[i, :, : heads * HD], acc_ref[i, :, heads * HD :].T[:8])


def write_share(ref, sums, totals):
    rows = sums.shape[0]
    ref[:rows] = sums.astype(jnp.bfloat16)
    pad = jnp.zeros((8, sums.shape[1] - rows), jnp.float32)
    high = totals.astype(jnp.bfloat16).astype(jnp.float32)
    low = totals - high
    both = jnp.concatenate(
        [jnp.concatenate([high, pad], axis=1), jnp.concatenate([low, pad], axis=1)], axis=0
    )
    ref[rows:] = both.astype(jnp.bfloat16)


def read_totals(ref, rows):
    both = ref[rows:, :rows].astype(jnp.float32)
    return both[:8] + both[8:]


def attend(qs, ks, vs, state, last):
    rows, width = qs[0].shape[0] - ID_ROWS, vs[0].shape[1]
    n_keys = len(ks)
    wide = width + HD
    vmem = pl.BlockSpec(memory_space=pltpu.VMEM)
    state_shape = jax.ShapeDtypeStruct((4, rows, wide), jnp.float32)
    if last:
        out_shape = [
            jax.ShapeDtypeStruct((2, rows, width), jnp.float32),
            jax.ShapeDtypeStruct((2, 8, rows), jnp.float32),
            jax.ShapeDtypeStruct((2, rows + ID_ROWS, width), jnp.bfloat16),
        ]
        scratch = [pltpu.VMEM((4, rows, wide), jnp.float32)]
    else:
        out_shape, scratch = [state_shape], []
    first = state is None
    args = [*qs, *ks, *vs] + ([] if first else [state])

    def body(*refs):
        attend_kernel(n_keys, first, last, *refs)

    flops = 4 * n_keys * 3 * rows * rows * HD * 4
    return pl.pallas_call(
        body,
        in_specs=[vmem] * len(args),
        out_specs=[vmem] * len(out_shape),
        out_shape=out_shape,
        scratch_shapes=scratch,
        compiler_params=pltpu.CompilerParams(vmem_limit_bytes=32 * MIB),
        cost_estimate=pl.CostEstimate(
            flops=flops, bytes_accessed=8 * MIB, transcendentals=4 * n_keys * 3 * rows * rows
        ),
        name="attend",
    )(*args)


def fold_kernel(keep_ref, sum_ref, got_ref, own_ref, own_sum, send_ref):
    rows = keep_ref.shape[1]
    own_ref[...] = keep_ref[0] + got_ref[0, :rows].astype(jnp.float32)
    own_sum[...] = sum_ref[0] + read_totals(got_ref.at[0], rows)
    write_share(
        send_ref,
        keep_ref[1] + got_ref[1, :rows].astype(jnp.float32),
        sum_ref[1] + read_totals(got_ref.at[1], rows),
    )


def fold(keep, sums, got):
    _, rows, width = keep.shape
    vmem = pl.BlockSpec(memory_space=pltpu.VMEM)
    return pl.pallas_call(
        fold_kernel,
        in_specs=[vmem] * 3,
        out_specs=[vmem] * 3,
        out_shape=[
            jax.ShapeDtypeStruct((rows, width), jnp.float32),
            jax.ShapeDtypeStruct((8, rows), jnp.float32),
            jax.ShapeDtypeStruct((rows + ID_ROWS, width), jnp.bfloat16),
        ],
        compiler_params=pltpu.CompilerParams(vmem_limit_bytes=8 * MIB),
        name="fold",
    )(keep, sums, got)


def finish_kernel(own_ref, sum_ref, got_ref, upper_ref, lower_ref):
    half, width = upper_ref.shape
    rows = 2 * half
    total = own_ref[...] + got_ref[:rows].astype(jnp.float32)
    sums = sum_ref[...] + read_totals(got_ref, rows)
    columns = jnp.concatenate([sums, jnp.ones((120, rows), jnp.float32)], axis=0).T
    for h in range(width // HD):
        cols = slice(h * HD, (h + 1) * HD)
        normed = (total[:, cols] / columns[:, h : h + 1]).astype(jnp.bfloat16)
        upper_ref[:, cols] = normed[:half]
        lower_ref[:, cols] = normed[half:]


def finish(own, sums, got):
    rows, width = own.shape
    vmem = pl.BlockSpec(memory_space=pltpu.VMEM)
    half = jax.ShapeDtypeStruct((rows // 2, width), jnp.bfloat16)
    return pl.pallas_call(
        finish_kernel,
        in_specs=[vmem] * 3,
        out_specs=[vmem] * 2,
        out_shape=[half, half],
        compiler_params=pltpu.CompilerParams(vmem_limit_bytes=8 * MIB),
        name="finish",
    )(own, sums, got)


def arrange_kernel(spot_ref, here_ref, early_own, late_own, early_mate, late_mate, out_ref):
    y_lo, core = here_ref[0], here_ref[1]
    for n in range(4):
        early, late = ((early_own, late_own), (early_mate, late_mate))[n // 2]
        far = n % 2
        part = lax.rem(core + n // 2, 2) * 2 + lax.rem(y_lo + far, 2)
        for s in range(8):
            out_ref[spot_ref[s], part] = early[far * 5 + s] if s < 5 else late[far * 3 + s - 5]


def arrange_weight(weights, spots, here):
    _, cols, width = weights[0].shape
    vmem = pl.BlockSpec(memory_space=pltpu.VMEM)
    return pl.pallas_call(
        arrange_kernel,
        in_specs=[pl.BlockSpec(memory_space=pltpu.SMEM)] * 2 + [vmem] * 4,
        out_specs=vmem,
        out_shape=jax.ShapeDtypeStruct((8, 4, cols, width), weights[0].dtype),
        compiler_params=pltpu.CompilerParams(vmem_limit_bytes=16 * MIB),
        cost_estimate=pl.CostEstimate(flops=0, bytes_accessed=8 * MIB, transcendentals=0),
        name="arrange",
    )(spots, here, *weights)


HERE, THERE = (0, 1, 2, 3), (4, 5, 6, 7)


def term_of(rows, w_ref, r):
    weight = w_ref[r].reshape(-1, rows.shape[1])
    return lax.dot_general(rows, weight, (((1,), (1,)), ((), ())), preferred_element_type=jnp.float32)


def project_kernel(b0, b1, b2, b3, along, w_ref, upper_ref, lower_ref):
    half = upper_ref.shape[0]
    upper = lower = None
    for n, both in enumerate((b0, b1, b2, b3)):
        for rows, r in ((both[:half], HERE[n]), (both[half:], THERE[n])):
            term = term_of(rows, w_ref, r)
            upper = term if upper is None else upper + term
        term = term_of(along[n * half : (n + 1) * half], w_ref, HERE[n])
        lower = term if lower is None else lower + term
    upper_ref[...] = upper.astype(jnp.bfloat16)
    lower_ref[...] = lower


def project_last_kernel(upper_ref, lower_ref, far, w_ref, out_ref):
    half = upper_ref.shape[0]
    out_ref[:half] = upper_ref[...]
    lower = lower_ref[...]
    for n in range(4):
        lower = lower + term_of(far[n * half : (n + 1) * half], w_ref, THERE[n])
    out_ref[half:] = lower.astype(jnp.bfloat16)


def project(both, along, far, weight):
    rows, width = both[0].shape
    half = rows // 2
    columns = weight.shape[1] * weight.shape[2]
    vmem = pl.BlockSpec(memory_space=pltpu.VMEM)

    def call(kernel, args, out_shape, terms):
        return pl.pallas_call(
            kernel,
            in_specs=[vmem] * len(args),
            out_specs=[vmem] * len(out_shape),
            out_shape=out_shape,
            compiler_params=pltpu.CompilerParams(vmem_limit_bytes=16 * MIB),
            cost_estimate=pl.CostEstimate(
                flops=2 * half * terms * width * columns, bytes_accessed=8 * width * columns * 2, transcendentals=0
            ),
            name="project",
        )(*args)

    upper, lower = call(
        project_kernel,
        [*both, along, weight],
        [
            jax.ShapeDtypeStruct((half, columns), jnp.bfloat16),
            jax.ShapeDtypeStruct((half, columns), jnp.float32),
        ],
        12,
    )
    return call(
        project_last_kernel,
        [upper, lower, far, weight],
        [jax.ShapeDtypeStruct((rows, columns), jnp.bfloat16)],
        4,
    )[0]


RING_SLOT = (0, 2, 4, 6, 7, 5, 3, 1)


def regroup_weight(out_weight):
    pairs = []
    for c in range(N_CTX):
        c_lo, c_z, c_core = c // 16, (c // 2) % N_Z, c % 2
        for t in range(N_TP):
            pairs.append(((4 * t + c_core * 2 + c_lo) * N_TP + c_z, c * N_TP + t))
    return lax.ppermute(out_weight.T, ("ctx", "tp"), pairs)


def on_device(tokens, qkv_weight, query_gain, key_gain, out_weight, block_ids):
    places = sender_places()
    c = lax.axis_index("ctx")
    here = jnp.stack([c // 16, c % 2]).astype(jnp.int32)
    distance = (places - (c // 2) % N_Z + N_Z) % N_Z
    slots = sum(jnp.where(distance == d, slot, 0) for d, slot in enumerate(RING_SLOT))
    step = jnp.arange(8, dtype=jnp.int32)
    spots = jnp.sum(jnp.where(slots[None, :] == step[:, None], step[None, :], 0), axis=1).astype(jnp.int32)

    out_block = regroup_weight(out_weight)
    half = tokens.shape[0] // 2
    weight = order_weight(qkv_weight.transpose(1, 0, 2), places)
    q_flat, k_flat, values, squares = qkv(
        *gather_tp(tokens[:half], tokens[half:]), weight, out_block
    )

    v_up, v_down = [values, move(values, z=1)], [values, move(values, z=-1)]
    pair_sum = squares + move(squares, y_hi=1)
    parts = [pair_sum] + [move(pair_sum, x=x) for x in (2, 1, 3)]
    queries, keys = norm(
        block_ids[:1], parts, after(q_flat, v_up[1], v_down[1]), k_flat, query_gain.reshape(1, -1), key_gain.reshape(1, -1)
    )

    mate = move(queries, core=1)
    across = move(queries, y_lo=1)
    qs = [queries, mate, across, move(across, core=1)]

    rows = block_ids.shape[0]
    for _ in range(2):
        v_up.append(move(v_up[-1], z=1))
        v_down.append(move(v_down[-1], z=-1))
    v_far = move(v_down[3], z=-1)
    early = jnp.stack([v[rows:] for v in (values, v_up[1], v_down[1], v_up[2], v_down[2])])
    late = jnp.stack([v[rows:] for v in (v_up[3], v_down[3], v_far)])
    early_far, late_far = move(after(early, across), y_lo=1), move(late, y_lo=1)

    k_up, k_down = [keys, move(keys, z=1)], [keys, move(keys, z=-1)]
    k_up.append(move(k_up[1], z=1))
    k_down.append(move(k_down[1], z=-1))
    (state,) = attend(qs, [keys, k_up[1], k_down[1]], [values, v_up[1], v_down[1]], None, False)
    k_up.append(move(after(k_up[2], state), z=1))
    k_down.append(move(after(k_down[2], state), z=-1))
    (state,) = attend(qs, [k_up[2], k_down[2]], [v_up[2], v_down[2]], state, False)
    k_far = move(after(k_up[3], state), z=1)
    (state,) = attend(qs, [k_up[3], k_down[3]], [v_up[3], v_down[3]], state, False)
    early_own = jnp.concatenate([early, early_far])
    early_mate = move(after(early_own, state), core=1)
    keep, sums, send = attend(qs, [k_far], [v_far], state, True)

    own, sums, send = fold(keep, sums, move(send, core=1))
    got = move(send, y_lo=1)
    late_own = jnp.concatenate([late, late_far])
    late_mate = move(after(late_own, got), core=1)
    upper, lower = finish(own, sums, got)
    both, along, far = gather_tp(upper, lower)
    out_whole = arrange_weight([early_own, late_own, early_mate, late_mate], spots, here)
    return project(both, along, far, out_whole)


def solution(mesh):
    in_specs = (P("ctx", "tp"), P(None, None, "tp"), P("tp"), P("tp"), P("tp", "ctx"), P("ctx"))
    out_specs = P("ctx", "tp")
    return jax.shard_map(
        on_device, mesh=mesh, in_specs=in_specs, out_specs=out_specs, check_vma=False
    )
```

```python
import math

import jax
import jax.numpy as jnp
from jax import lax
from jax.experimental import pallas as pl
from jax.experimental.pallas import tpu as pltpu
from jax.sharding import PartitionSpec as P

HEADS = 24
HD = 128
ID_ROWS = 16
N_Z = 8
N_X = 4
N_TP = 8
N_CTX = 32
MIB = 1 << 20


def move(value, x=0, y_hi=0, y_lo=0, z=0, core=0):
    pairs = []
    for c in range(N_CTX):
        for t in range(N_TP):
            c_lo, c_z, c_core = c // 16, (c // 2) % 8, c % 2
            t_x, t_hi = t // 2, t % 2
            dst_c = ((c_lo + y_lo) % 2) * 16 + ((c_z + z) % N_Z) * 2 + (c_core + core) % 2
            dst_t = ((t_x + x) % N_X) * 2 + (t_hi + y_hi) % 2
            pairs.append((c * N_TP + t, dst_c * N_TP + dst_t))
    return lax.ppermute(value, ("ctx", "tp"), pairs)


TP_STEPS = [(0, 0), (1, 0), (3, 0), (2, 0), (0, 1), (1, 1), (3, 1), (2, 1)]


def after(value, *others):
    return lax.optimization_barrier((value, *others))[0]


def gather_tp(upper, lower):
    both = jnp.concatenate([upper, move(upper, y_hi=1)])
    along = jnp.concatenate([lower] + [move(lower, x=x) for x in (1, 3, 2)])
    far = move(along, y_hi=1)
    return [both] + [move(both, x=x) for x in (1, 3, 2)], along, far


def sender_places():
    t = lax.axis_index("tp")
    t_x, t_hi = t // 2, t % 2
    places = [((t_x - x + N_X) % N_X) * 2 + (t_hi - y_hi + 2) % 2 for x, y_hi in TP_STEPS]
    return jnp.stack(places + [lax.axis_index("ctx")]).astype(jnp.int32)


def order_kernel(place_ref, w_ref, out_ref, sems):
    feats = out_ref.shape[1] // 8

    def fetch(r):
        start = pl.multiple_of(place_ref[r] * feats, feats)
        return pltpu.make_async_copy(
            w_ref.at[:, pl.ds(start, feats), :], out_ref.at[:, pl.ds(r * feats, feats), :], sems.at[r]
        )

    for r in range(8):
        fetch(r).start()
    for r in range(8):
        fetch(r).wait()


def order_weight(weight, places):
    return pl.pallas_call(
        order_kernel,
        in_specs=[pl.BlockSpec(memory_space=pltpu.SMEM), pl.BlockSpec(memory_space=pl.ANY)],
        out_specs=pl.BlockSpec(memory_space=pltpu.VMEM),
        out_shape=jax.ShapeDtypeStruct(weight.shape, weight.dtype),
        scratch_shapes=[pltpu.SemaphoreType.DMA((8,))],
        compiler_params=pltpu.CompilerParams(vmem_limit_bytes=32 * MIB),
        cost_estimate=pl.CostEstimate(flops=0, bytes_accessed=24 * MIB, transcendentals=0),
        name="order",
    )(places, weight)


def product(rows, w_ref, p, block):
    wide = jnp.concatenate(rows, axis=1) if len(rows) > 1 else rows[0]
    feats = w_ref.shape[1] // 8
    return jnp.dot(
        wide, w_ref[p, block * feats : block * feats + wide.shape[1], :], preferred_element_type=jnp.float32
    )


def lower_kernel(block, *refs):
    held, w_ref, out_ref = refs[0], refs[-2], refs[-1]
    half = held.shape[0] // 4
    rows = [held[n * half : (n + 1) * half] for n in range(4)]
    for p in range(3):
        term = product(rows, w_ref, p, block)
        out_ref[p] = term if block == 0 else refs[1][p] + term


def upper_kernel(b0, b1, b2, w_ref, out_ref):
    half = b0.shape[0] // 2
    for p in range(3):
        here = product([b[:half] for b in (b0, b1, b2)], w_ref, p, 0)
        out_ref[p] = here + product([b[half:] for b in (b0, b1, b2)], w_ref, p, 4)


def last_kernel(b3, upper_ref, lower_ref, w_ref, out_w, q_ref, k_ref, v_ref, sq_ref):
    half = b3.shape[0] // 2

    def whole(p):
        upper = upper_ref[p] + product([b3[:half]], w_ref, p, 3) + product([b3[half:]], w_ref, p, 7)
        return jnp.concatenate([upper, lower_ref[p]], axis=0)

    q, k, v = [whole(p) for p in range(3)]
    q_ref[...] = q
    k_ref[...] = k
    v_ref[: v.shape[0]] = v.astype(jnp.bfloat16)
    v_ref[v.shape[0] :] = out_w[...]
    q_sq = jnp.sum(q * q, axis=1, keepdims=True)
    k_sq = jnp.sum(k * k, axis=1, keepdims=True)
    lane = lax.broadcasted_iota(jnp.int32, (q.shape[0], 128), 1)
    both = jnp.where(lane == 0, q_sq, jnp.where(lane == 1, k_sq, 0.0))
    sq_ref[...] = both.T[:8]


def qkv(firsts, along, far, weight, out_block):
    rows, feats = firsts[0].shape
    half = rows // 2
    width = weight.shape[2]
    vmem = pl.BlockSpec(memory_space=pltpu.VMEM)
    share = jax.ShapeDtypeStruct((3, half, width), jnp.float32)

    def call(kernel, args, out_shape, blocks):
        return pl.pallas_call(
            kernel,
            in_specs=[vmem] * len(args),
            out_specs=[vmem] * len(out_shape),
            out_shape=out_shape,
            compiler_params=pltpu.CompilerParams(vmem_limit_bytes=32 * MIB),
            cost_estimate=pl.CostEstimate(
                flops=2 * half * blocks * feats * 3 * width,
                bytes_accessed=blocks * feats * 3 * width * 2,
                transcendentals=0,
            ),
            name="qkv",
        )(*args)

    def lower_part(block, *args):
        return call(lambda *refs: lower_kernel(block, *refs), [*args, weight], [share], 4)[0]

    lower = lower_part(0, along)
    lower = lower_part(4, far, lower)
    (upper,) = call(upper_kernel, [*firsts[:3], weight], [share], 6)
    whole = jax.ShapeDtypeStruct((rows, width), jnp.float32)
    return call(
        last_kernel,
        [firsts[3], upper, lower, weight, out_block],
        [
            whole,
            whole,
            jax.ShapeDtypeStruct((rows + out_block.shape[0], width), jnp.bfloat16),
            jax.ShapeDtypeStruct((8, rows), jnp.float32),
        ],
        2,
    )


def norm_kernel(id_ref, s0, s1, s2, s3, q_ref, k_ref, qg_ref, kg_ref, q_out, k_out):
    rows = q_ref.shape[0]
    total = s0[...] + s1[...] + s2[...] + s3[...]
    inverse = lax.rsqrt(total * (1.0 / (HEADS * HD)) + 1e-06)
    columns = jnp.concatenate([inverse, jnp.zeros((120, rows), jnp.float32)], axis=0).T
    q_scale = math.log2(math.e) / math.sqrt(HD)
    q_out[:rows] = (q_ref[...] * columns[:, 0:1] * (qg_ref[...] * q_scale)).astype(jnp.bfloat16)
    k_out[:rows] = (k_ref[...] * columns[:, 1:2] * kg_ref[...]).astype(jnp.bfloat16)
    span = jnp.full((ID_ROWS, q_ref.shape[1]), id_ref[0].astype(jnp.float32), jnp.float32)
    q_out[rows:] = span.astype(jnp.bfloat16)
    k_out[rows:] = span.astype(jnp.bfloat16)


def norm(span_id, squares, q, k, q_gain, k_gain):
    rows, width = q.shape
    vmem = pl.BlockSpec(memory_space=pltpu.VMEM)
    out = jax.ShapeDtypeStruct((rows + ID_ROWS, width), jnp.bfloat16)
    return pl.pallas_call(
        norm_kernel,
        in_specs=[pl.BlockSpec(memory_space=pltpu.SMEM)] + [vmem] * 8,
        out_specs=[vmem] * 2,
        out_shape=[out, out],
        compiler_params=pltpu.CompilerParams(vmem_limit_bytes=12 * MIB),
        name="norm",
    )(span_id, *squares, q, k, q_gain, k_gain)


def attend_kernel(n_keys, first, last, *refs):
    qs, ks, vs = refs[:4], refs[4 : 4 + n_keys], refs[4 + n_keys : 4 + 2 * n_keys]
    rest = refs[4 + 2 * n_keys :]
    rows = qs[0].shape[0] - ID_ROWS
    heads = vs[0].shape[1] // HD
    if first:
        acc_ref, = rest[:1]
        acc_ref[...] = jnp.zeros_like(acc_ref)
    elif last:
        acc_in, keep_ref, keep_sum, send_ref, acc_ref = rest
        acc_ref[...] = acc_in[...]
    else:
        acc_in, acc_ref = rest
        acc_ref[...] = acc_in[...]
    lane = lax.broadcasted_iota(jnp.int32, (rows, HD), 1)
    ones = jnp.ones((rows, HD), jnp.bfloat16)
    q_ids = [jnp.max(q[rows:, :HD].astype(jnp.float32)) for q in qs]
    k_ids = [jnp.max(k[rows:, :HD].astype(jnp.float32)) for k in ks]
    for i in range(4):
        for j in range(n_keys):

            @pl.when(k_ids[j] <= q_ids[i])
            def _():
                sums = None
                for h in range(heads):
                    cols = slice(h * HD, (h + 1) * HD)
                    scores = lax.dot_general(
                        qs[i][:rows, cols], ks[j][:rows, cols], (((1,), (1,)), ((), ())),
                        preferred_element_type=jnp.float32,
                    )
                    weights = jnp.exp2(scores).astype(jnp.bfloat16)
                    wide = jnp.concatenate([vs[j][:rows, cols], ones], axis=1)
                    both = jnp.dot(weights, wide, preferred_element_type=jnp.float32)
                    acc_ref[i, :, cols] += both[:, :HD]
                    sums = both[:, HD:] if h == 0 else jnp.where(lane == h, both[:, HD:], sums)
                acc_ref[i, :, heads * HD :] += sums
    if last:
        for n, i in enumerate((0, 2)):
            keep_ref[n] = acc_ref[i, :, : heads * HD]
            keep_sum[n] = acc_ref[i, :, heads * HD :].T[:8]
        for n, i in enumerate((1, 3)):
            write_share(send_ref.at[n], acc_ref[i, :, : heads * HD], acc_ref[i, :, heads * HD :].T[:8])


def write_share(ref, sums, totals):
    rows = sums.shape[0]
    ref[:rows] = sums.astype(jnp.bfloat16)
    pad = jnp.zeros((8, sums.shape[1] - rows), jnp.float32)
    high = totals.astype(jnp.bfloat16).astype(jnp.float32)
    low = totals - high
    both = jnp.concatenate(
        [jnp.concatenate([high, pad], axis=1), jnp.concatenate([low, pad], axis=1)], axis=0
    )
    ref[rows:] = both.astype(jnp.bfloat16)


def read_totals(ref, rows):
    both = ref[rows:, :rows].astype(jnp.float32)
    return both[:8] + both[8:]


def attend(qs, ks, vs, state, last):
    rows, width = qs[0].shape[0] - ID_ROWS, vs[0].shape[1]
    n_keys = len(ks)
    wide = width + HD
    vmem = pl.BlockSpec(memory_space=pltpu.VMEM)
    state_shape = jax.ShapeDtypeStruct((4, rows, wide), jnp.float32)
    if last:
        out_shape = [
            jax.ShapeDtypeStruct((2, rows, width), jnp.float32),
            jax.ShapeDtypeStruct((2, 8, rows), jnp.float32),
            jax.ShapeDtypeStruct((2, rows + ID_ROWS, width), jnp.bfloat16),
        ]
        scratch = [pltpu.VMEM((4, rows, wide), jnp.float32)]
    else:
        out_shape, scratch = [state_shape], []
    first = state is None
    args = [*qs, *ks, *vs] + ([] if first else [state])

    def body(*refs):
        attend_kernel(n_keys, first, last, *refs)

    flops = 4 * n_keys * 3 * rows * rows * HD * 4
    return pl.pallas_call(
        body,
        in_specs=[vmem] * len(args),
        out_specs=[vmem] * len(out_shape),
        out_shape=out_shape,
        scratch_shapes=scratch,
        compiler_params=pltpu.CompilerParams(vmem_limit_bytes=32 * MIB),
        cost_estimate=pl.CostEstimate(
            flops=flops, bytes_accessed=8 * MIB, transcendentals=4 * n_keys * 3 * rows * rows
        ),
        name="attend",
    )(*args)


def fold_kernel(keep_ref, sum_ref, got_ref, own_ref, own_sum, send_ref):
    rows = keep_ref.shape[1]
    own_ref[...] = keep_ref[0] + got_ref[0, :rows].astype(jnp.float32)
    own_sum[...] = sum_ref[0] + read_totals(got_ref.at[0], rows)
    write_share(
        send_ref,
        keep_ref[1] + got_ref[1, :rows].astype(jnp.float32),
        sum_ref[1] + read_totals(got_ref.at[1], rows),
    )


def fold(keep, sums, got):
    _, rows, width = keep.shape
    vmem = pl.BlockSpec(memory_space=pltpu.VMEM)
    return pl.pallas_call(
        fold_kernel,
        in_specs=[vmem] * 3,
        out_specs=[vmem] * 3,
        out_shape=[
            jax.ShapeDtypeStruct((rows, width), jnp.float32),
            jax.ShapeDtypeStruct((8, rows), jnp.float32),
            jax.ShapeDtypeStruct((rows + ID_ROWS, width), jnp.bfloat16),
        ],
        compiler_params=pltpu.CompilerParams(vmem_limit_bytes=8 * MIB),
        name="fold",
    )(keep, sums, got)


def finish_kernel(own_ref, sum_ref, got_ref, upper_ref, lower_ref):
    half, width = upper_ref.shape
    rows = 2 * half
    total = own_ref[...] + got_ref[:rows].astype(jnp.float32)
    sums = sum_ref[...] + read_totals(got_ref, rows)
    columns = jnp.concatenate([sums, jnp.ones((120, rows), jnp.float32)], axis=0).T
    for h in range(width // HD):
        cols = slice(h * HD, (h + 1) * HD)
        normed = (total[:, cols] / columns[:, h : h + 1]).astype(jnp.bfloat16)
        upper_ref[:, cols] = normed[:half]
        lower_ref[:, cols] = normed[half:]


def finish(own, sums, got):
    rows, width = own.shape
    vmem = pl.BlockSpec(memory_space=pltpu.VMEM)
    half = jax.ShapeDtypeStruct((rows // 2, width), jnp.bfloat16)
    return pl.pallas_call(
        finish_kernel,
        in_specs=[vmem] * 3,
        out_specs=[vmem] * 2,
        out_shape=[half, half],
        compiler_params=pltpu.CompilerParams(vmem_limit_bytes=8 * MIB),
        name="finish",
    )(own, sums, got)


def arrange_kernel(place_ref, own_ref, mate_ref, out_ref):
    c = place_ref[8]
    y_lo, z, core = c // 16, lax.rem(c // 2, N_Z), lax.rem(c, 2)
    for r in range(8):
        distance = lax.rem(place_ref[r] - z + N_Z, N_Z)
        slot = 0
        for d, held in enumerate(RING_SLOT):
            slot = jnp.where(distance == d, held, slot)
        for n in range(4):
            held, far = (own_ref, mate_ref)[n // 2], n % 2
            part = lax.rem(core + n // 2, 2) * 2 + lax.rem(y_lo + far, 2)
            out_ref[r, part] = held[far * 8 + slot]


def arrange_weight(own, mate, places):
    _, cols, width = own.shape
    vmem = pl.BlockSpec(memory_space=pltpu.VMEM)
    return pl.pallas_call(
        arrange_kernel,
        in_specs=[pl.BlockSpec(memory_space=pltpu.SMEM)] + [vmem] * 2,
        out_specs=vmem,
        out_shape=jax.ShapeDtypeStruct((8, 4, cols, width), own.dtype),
        compiler_params=pltpu.CompilerParams(vmem_limit_bytes=16 * MIB),
        cost_estimate=pl.CostEstimate(flops=0, bytes_accessed=8 * MIB, transcendentals=0),
        name="arrange",
    )(places, own, mate)


HERE, THERE = (0, 1, 2, 3), (4, 5, 6, 7)


def term_of(rows, w_ref, r):
    weight = w_ref[r].reshape(-1, rows.shape[1])
    return lax.dot_general(rows, weight, (((1,), (1,)), ((), ())), preferred_element_type=jnp.float32)


def project_kernel(b0, b1, b2, b3, along, w_ref, upper_ref, lower_ref):
    half = upper_ref.shape[0]
    upper = lower = None
    for n, both in enumerate((b0, b1, b2, b3)):
        for rows, r in ((both[:half], HERE[n]), (both[half:], THERE[n])):
            term = term_of(rows, w_ref, r)
            upper = term if upper is None else upper + term
        term = term_of(along[n * half : (n + 1) * half], w_ref, HERE[n])
        lower = term if lower is None else lower + term
    upper_ref[...] = upper.astype(jnp.bfloat16)
    lower_ref[...] = lower


def project_last_kernel(upper_ref, lower_ref, far, w_ref, out_ref):
    half = upper_ref.shape[0]
    out_ref[:half] = upper_ref[...]
    lower = lower_ref[...]
    for n in range(4):
        lower = lower + term_of(far[n * half : (n + 1) * half], w_ref, THERE[n])
    out_ref[half:] = lower.astype(jnp.bfloat16)


def project(both, along, far, weight):
    rows, width = both[0].shape
    half = rows // 2
    columns = weight.shape[1] * weight.shape[2]
    vmem = pl.BlockSpec(memory_space=pltpu.VMEM)

    def call(kernel, args, out_shape, terms):
        return pl.pallas_call(
            kernel,
            in_specs=[vmem] * len(args),
            out_specs=[vmem] * len(out_shape),
            out_shape=out_shape,
            compiler_params=pltpu.CompilerParams(vmem_limit_bytes=16 * MIB),
            cost_estimate=pl.CostEstimate(
                flops=2 * half * terms * width * columns, bytes_accessed=8 * width * columns * 2, transcendentals=0
            ),
            name="project",
        )(*args)

    upper, lower = call(
        project_kernel,
        [*both, along, weight],
        [
            jax.ShapeDtypeStruct((half, columns), jnp.bfloat16),
            jax.ShapeDtypeStruct((half, columns), jnp.float32),
        ],
        12,
    )
    return call(
        project_last_kernel,
        [upper, lower, far, weight],
        [jax.ShapeDtypeStruct((rows, columns), jnp.bfloat16)],
        4,
    )[0]


RING_SLOT = (0, 2, 4, 6, 7, 5, 3, 1)


def regroup_weight(out_weight):
    pairs = []
    for c in range(N_CTX):
        c_lo, c_z, c_core = c // 16, (c // 2) % N_Z, c % 2
        for t in range(N_TP):
            pairs.append(((4 * t + c_core * 2 + c_lo) * N_TP + c_z, c * N_TP + t))
    return lax.ppermute(out_weight.T, ("ctx", "tp"), pairs)


def on_device(tokens, qkv_weight, query_gain, key_gain, out_weight, block_ids):
    places = sender_places()
    out_block = regroup_weight(out_weight)
    half = tokens.shape[0] // 2
    weight = order_weight(qkv_weight.transpose(1, 0, 2), places)
    q_flat, k_flat, values, squares = qkv(
        *gather_tp(tokens[:half], tokens[half:]), weight, out_block
    )

    pair_sum = squares + move(squares, y_hi=1)
    tied = after(values, pair_sum)
    v_up, v_down = [values, move(tied, z=1)], [values, move(tied, z=-1)]
    parts = [pair_sum] + [move(pair_sum, x=x) for x in (2, 1, 3)]
    queries, keys = norm(
        block_ids, parts, after(q_flat, v_up[1], v_down[1]), k_flat, query_gain.reshape(1, -1), key_gain.reshape(1, -1)
    )

    mate = move(queries, core=1)
    across = move(queries, y_lo=1)
    qs = [queries, mate, across, move(across, core=1)]

    rows = block_ids.shape[0]
    for _ in range(2):
        v_up.append(move(v_up[-1], z=1))
        v_down.append(move(v_down[-1], z=-1))
    v_far = move(v_down[3], z=-1)
    first = jnp.stack([v[rows:] for v in (values, v_up[1], v_down[1])])
    middle = jnp.stack([v[rows:] for v in (v_up[2], v_down[2], v_up[3], v_down[3])])
    first_far, middle_far = move(after(first, across), y_lo=1), move(middle, y_lo=1)

    k_up, k_down = [keys, move(keys, z=1)], [keys, move(keys, z=-1)]
    k_up.append(move(k_up[1], z=1))
    k_down.append(move(k_down[1], z=-1))
    (state,) = attend(qs, [keys, k_up[1], k_down[1]], [values, v_up[1], v_down[1]], None, False)
    k_up.append(move(after(k_up[2], state), z=1))
    k_down.append(move(after(k_down[2], state), z=-1))
    (state,) = attend(qs, [k_up[2], k_down[2]], [v_up[2], v_down[2]], state, False)
    k_far = move(after(k_up[3], state), z=1)
    (state,) = attend(qs, [k_up[3], k_down[3]], [v_up[3], v_down[3]], state, False)
    keep, sums, send = attend(qs, [k_far], [v_far], state, True)

    own, sums, send = fold(keep, sums, move(send, core=1))
    got = move(send, y_lo=1)
    late = v_far[None, rows:]
    out_own = jnp.concatenate([first, middle, late, first_far, middle_far, move(late, y_lo=1)])
    out_mate = move(after(out_own, got), core=1)
    upper, lower = finish(own, sums, got)
    both, along, far = gather_tp(upper, lower)
    out_whole = arrange_weight(out_own, out_mate, places)
    return project(both, along, far, out_whole)


def solution(mesh):
    in_specs = (P("ctx", "tp"), P(None, None, "tp"), P("tp"), P("tp"), P("tp", "ctx"), P("ctx"))
    out_specs = P("ctx", "tp")
    return jax.shard_map(
        on_device, mesh=mesh, in_specs=in_specs, out_specs=out_specs, check_vma=False
    )
```

```python
import math

import jax
import jax.numpy as jnp
from jax import lax
from jax.experimental import pallas as pl
from jax.experimental.pallas import tpu as pltpu
from jax.sharding import PartitionSpec as P

HEADS = 24
HD = 128
ID_ROWS = 16
N_Z = 8
N_X = 4
N_TP = 8
N_CTX = 32
MIB = 1 << 20


def move(value, x=0, y_hi=0, y_lo=0, z=0, core=0):
    pairs = []
    for c in range(N_CTX):
        for t in range(N_TP):
            c_lo, c_z, c_core = c // 16, (c // 2) % 8, c % 2
            t_x, t_hi = t // 2, t % 2
            dst_c = ((c_lo + y_lo) % 2) * 16 + ((c_z + z) % N_Z) * 2 + (c_core + core) % 2
            dst_t = ((t_x + x) % N_X) * 2 + (t_hi + y_hi) % 2
            pairs.append((c * N_TP + t, dst_c * N_TP + dst_t))
    return lax.ppermute(value, ("ctx", "tp"), pairs)


TP_STEPS = [(0, 0), (1, 0), (3, 0), (2, 0), (0, 1), (1, 1), (3, 1), (2, 1)]


def after(value, *others):
    return lax.optimization_barrier((value, *others))[0]


def gather_tp(upper, lower):
    both = jnp.concatenate([upper, move(upper, y_hi=1)])
    along = jnp.concatenate([lower] + [move(lower, x=x) for x in (1, 3, 2)])
    far = move(along, y_hi=1)
    return [both] + [move(both, x=x) for x in (1, 3, 2)], along, far


def sender_places():
    t = lax.axis_index("tp")
    t_x, t_hi = t // 2, t % 2
    places = [((t_x - x + N_X) % N_X) * 2 + (t_hi - y_hi + 2) % 2 for x, y_hi in TP_STEPS]
    return jnp.stack(places + [lax.axis_index("ctx")]).astype(jnp.int32)


def order_kernel(place_ref, w_ref, out_ref, sems):
    feats = out_ref.shape[1] // 8

    def fetch(r):
        start = pl.multiple_of(place_ref[r] * feats, feats)
        return pltpu.make_async_copy(
            w_ref.at[:, pl.ds(start, feats), :], out_ref.at[:, pl.ds(r * feats, feats), :], sems.at[r]
        )

    for r in range(8):
        fetch(r).start()
    for r in range(8):
        fetch(r).wait()


def order_weight(weight, places):
    return pl.pallas_call(
        order_kernel,
        in_specs=[pl.BlockSpec(memory_space=pltpu.SMEM), pl.BlockSpec(memory_space=pl.ANY)],
        out_specs=pl.BlockSpec(memory_space=pltpu.VMEM),
        out_shape=jax.ShapeDtypeStruct(weight.shape, weight.dtype),
        scratch_shapes=[pltpu.SemaphoreType.DMA((8,))],
        compiler_params=pltpu.CompilerParams(vmem_limit_bytes=32 * MIB),
        cost_estimate=pl.CostEstimate(flops=0, bytes_accessed=24 * MIB, transcendentals=0),
        name="order",
    )(places, weight)


def product(rows, w_ref, p, block):
    wide = jnp.concatenate(rows, axis=1) if len(rows) > 1 else rows[0]
    feats = w_ref.shape[1] // 8
    return jnp.dot(
        wide, w_ref[p, block * feats : block * feats + wide.shape[1], :], preferred_element_type=jnp.float32
    )


def lower_kernel(block, *refs):
    held, w_ref, out_ref = refs[0], refs[-2], refs[-1]
    half = held.shape[0] // 4
    rows = [held[n * half : (n + 1) * half] for n in range(4)]
    for p in range(3):
        term = product(rows, w_ref, p, block)
        out_ref[p] = term if block == 0 else refs[1][p] + term


def upper_kernel(b0, b1, b2, w_ref, out_ref):
    half = b0.shape[0] // 2
    for p in range(3):
        here = product([b[:half] for b in (b0, b1, b2)], w_ref, p, 0)
        out_ref[p] = here + product([b[half:] for b in (b0, b1, b2)], w_ref, p, 4)


def last_kernel(b3, upper_ref, lower_ref, w_ref, out_w, q_ref, k_ref, v_ref, sq_ref):
    half = b3.shape[0] // 2

    def whole(p):
        upper = upper_ref[p] + product([b3[:half]], w_ref, p, 3) + product([b3[half:]], w_ref, p, 7)
        return jnp.concatenate([upper, lower_ref[p]], axis=0)

    q, k, v = [whole(p) for p in range(3)]
    q_ref[...] = q
    k_ref[...] = k
    v_ref[: v.shape[0]] = v.astype(jnp.bfloat16)
    v_ref[v.shape[0] :] = out_w[...]
    q_sq = jnp.sum(q * q, axis=1, keepdims=True)
    k_sq = jnp.sum(k * k, axis=1, keepdims=True)
    lane = lax.broadcasted_iota(jnp.int32, (q.shape[0], 128), 1)
    both = jnp.where(lane == 0, q_sq, jnp.where(lane == 1, k_sq, 0.0))
    sq_ref[...] = both.T[:8]


def qkv(firsts, along, far, weight, out_block):
    rows, feats = firsts[0].shape
    half = rows // 2
    width = weight.shape[2]
    vmem = pl.BlockSpec(memory_space=pltpu.VMEM)
    share = jax.ShapeDtypeStruct((3, half, width), jnp.float32)

    def call(kernel, args, out_shape, blocks):
        return pl.pallas_call(
            kernel,
            in_specs=[vmem] * len(args),
            out_specs=[vmem] * len(out_shape),
            out_shape=out_shape,
            compiler_params=pltpu.CompilerParams(vmem_limit_bytes=32 * MIB),
            cost_estimate=pl.CostEstimate(
                flops=2 * half * blocks * feats * 3 * width,
                bytes_accessed=blocks * feats * 3 * width * 2,
                transcendentals=0,
            ),
            name="qkv",
        )(*args)

    def lower_part(block, *args):
        return call(lambda *refs: lower_kernel(block, *refs), [*args, weight], [share], 4)[0]

    lower = lower_part(0, along)
    lower = lower_part(4, far, lower)
    (upper,) = call(upper_kernel, [*firsts[:3], weight], [share], 6)
    whole = jax.ShapeDtypeStruct((rows, width), jnp.float32)
    return call(
        last_kernel,
        [firsts[3], upper, lower, weight, out_block],
        [
            whole,
            whole,
            jax.ShapeDtypeStruct((rows + out_block.shape[0], width), jnp.bfloat16),
            jax.ShapeDtypeStruct((8, rows), jnp.float32),
        ],
        2,
    )


def norm_kernel(id_ref, s0, s1, s2, s3, q_ref, k_ref, qg_ref, kg_ref, q_out, k_out):
    rows = q_ref.shape[0]
    total = s0[...] + s1[...] + s2[...] + s3[...]
    inverse = lax.rsqrt(total * (1.0 / (HEADS * HD)) + 1e-06)
    columns = jnp.concatenate([inverse, jnp.zeros((120, rows), jnp.float32)], axis=0).T
    q_scale = math.log2(math.e) / math.sqrt(HD)
    q_out[:rows] = (q_ref[...] * columns[:, 0:1] * (qg_ref[...] * q_scale)).astype(jnp.bfloat16)
    k_out[:rows] = (k_ref[...] * columns[:, 1:2] * kg_ref[...]).astype(jnp.bfloat16)
    span = jnp.full((ID_ROWS, q_ref.shape[1]), id_ref[0].astype(jnp.float32), jnp.float32)
    q_out[rows:] = span.astype(jnp.bfloat16)
    k_out[rows:] = span.astype(jnp.bfloat16)


def norm(span_id, squares, q, k, q_gain, k_gain):
    rows, width = q.shape
    vmem = pl.BlockSpec(memory_space=pltpu.VMEM)
    out = jax.ShapeDtypeStruct((rows + ID_ROWS, width), jnp.bfloat16)
    return pl.pallas_call(
        norm_kernel,
        in_specs=[pl.BlockSpec(memory_space=pltpu.SMEM)] + [vmem] * 8,
        out_specs=[vmem] * 2,
        out_shape=[out, out],
        compiler_params=pltpu.CompilerParams(vmem_limit_bytes=12 * MIB),
        name="norm",
    )(span_id, *squares, q, k, q_gain, k_gain)


def attend_kernel(n_keys, first, last, *refs):
    qs, ks, vs = refs[:4], refs[4 : 4 + n_keys], refs[4 + n_keys : 4 + 2 * n_keys]
    rest = refs[4 + 2 * n_keys :]
    rows = qs[0].shape[0] - ID_ROWS
    heads = vs[0].shape[1] // HD
    if first:
        acc_ref, = rest[:1]
        acc_ref[...] = jnp.zeros_like(acc_ref)
    elif last:
        acc_in, keep_ref, keep_sum, send_ref, acc_ref = rest
        acc_ref[...] = acc_in[...]
    else:
        acc_in, acc_ref = rest
        acc_ref[...] = acc_in[...]
    lane = lax.broadcasted_iota(jnp.int32, (rows, HD), 1)
    ones = jnp.ones((rows, HD), jnp.bfloat16)
    q_ids = [jnp.max(q[rows:, :HD].astype(jnp.float32)) for q in qs]
    k_ids = [jnp.max(k[rows:, :HD].astype(jnp.float32)) for k in ks]
    for i in range(4):
        for j in range(n_keys):

            @pl.when(k_ids[j] <= q_ids[i])
            def _():
                sums = None
                for h in range(heads):
                    cols = slice(h * HD, (h + 1) * HD)
                    scores = lax.dot_general(
                        qs[i][:rows, cols], ks[j][:rows, cols], (((1,), (1,)), ((), ())),
                        preferred_element_type=jnp.float32,
                    )
                    weights = jnp.exp2(scores).astype(jnp.bfloat16)
                    wide = jnp.concatenate([vs[j][:rows, cols], ones], axis=1)
                    both = jnp.dot(weights, wide, preferred_element_type=jnp.float32)
                    acc_ref[i, :, cols] += both[:, :HD]
                    sums = both[:, HD:] if h == 0 else jnp.where(lane == h, both[:, HD:], sums)
                acc_ref[i, :, heads * HD :] += sums
    if last:
        for n, i in enumerate((0, 2)):
            keep_ref[n] = acc_ref[i, :, : heads * HD]
            keep_sum[n] = acc_ref[i, :, heads * HD :].T[:8]
        for n, i in enumerate((1, 3)):
            write_share(send_ref.at[n], acc_ref[i, :, : heads * HD], acc_ref[i, :, heads * HD :].T[:8])


def write_share(ref, sums, totals):
    rows = sums.shape[0]
    ref[:rows] = sums.astype(jnp.bfloat16)
    pad = jnp.zeros((8, sums.shape[1] - rows), jnp.float32)
    high = totals.astype(jnp.bfloat16).astype(jnp.float32)
    low = totals - high
    both = jnp.concatenate(
        [jnp.concatenate([high, pad], axis=1), jnp.concatenate([low, pad], axis=1)], axis=0
    )
    ref[rows:] = both.astype(jnp.bfloat16)


def read_totals(ref, rows):
    both = ref[rows:, :rows].astype(jnp.float32)
    return both[:8] + both[8:]


def attend(qs, ks, vs, state, last):
    rows, width = qs[0].shape[0] - ID_ROWS, vs[0].shape[1]
    n_keys = len(ks)
    wide = width + HD
    vmem = pl.BlockSpec(memory_space=pltpu.VMEM)
    state_shape = jax.ShapeDtypeStruct((4, rows, wide), jnp.float32)
    if last:
        out_shape = [
            jax.ShapeDtypeStruct((2, rows, width), jnp.float32),
            jax.ShapeDtypeStruct((2, 8, rows), jnp.float32),
            jax.ShapeDtypeStruct((2, rows + ID_ROWS, width), jnp.bfloat16),
        ]
        scratch = [pltpu.VMEM((4, rows, wide), jnp.float32)]
    else:
        out_shape, scratch = [state_shape], []
    first = state is None
    args = [*qs, *ks, *vs] + ([] if first else [state])

    def body(*refs):
        attend_kernel(n_keys, first, last, *refs)

    flops = 4 * n_keys * 3 * rows * rows * HD * 4
    return pl.pallas_call(
        body,
        in_specs=[vmem] * len(args),
        out_specs=[vmem] * len(out_shape),
        out_shape=out_shape,
        scratch_shapes=scratch,
        compiler_params=pltpu.CompilerParams(vmem_limit_bytes=32 * MIB),
        cost_estimate=pl.CostEstimate(
            flops=flops, bytes_accessed=8 * MIB, transcendentals=4 * n_keys * 3 * rows * rows
        ),
        name="attend",
    )(*args)


def fold_kernel(keep_ref, sum_ref, got_ref, own_ref, own_sum, send_ref):
    rows = keep_ref.shape[1]
    own_ref[...] = keep_ref[0] + got_ref[0, :rows].astype(jnp.float32)
    own_sum[...] = sum_ref[0] + read_totals(got_ref.at[0], rows)
    write_share(
        send_ref,
        keep_ref[1] + got_ref[1, :rows].astype(jnp.float32),
        sum_ref[1] + read_totals(got_ref.at[1], rows),
    )


def fold(keep, sums, got):
    _, rows, width = keep.shape
    vmem = pl.BlockSpec(memory_space=pltpu.VMEM)
    return pl.pallas_call(
        fold_kernel,
        in_specs=[vmem] * 3,
        out_specs=[vmem] * 3,
        out_shape=[
            jax.ShapeDtypeStruct((rows, width), jnp.float32),
            jax.ShapeDtypeStruct((8, rows), jnp.float32),
            jax.ShapeDtypeStruct((rows + ID_ROWS, width), jnp.bfloat16),
        ],
        compiler_params=pltpu.CompilerParams(vmem_limit_bytes=8 * MIB),
        name="fold",
    )(keep, sums, got)


def finish_kernel(own_ref, sum_ref, got_ref, upper_ref, lower_ref):
    half, width = upper_ref.shape
    rows = 2 * half
    total = own_ref[...] + got_ref[:rows].astype(jnp.float32)
    sums = sum_ref[...] + read_totals(got_ref, rows)
    columns = jnp.concatenate([sums, jnp.ones((120, rows), jnp.float32)], axis=0).T
    for h in range(width // HD):
        cols = slice(h * HD, (h + 1) * HD)
        normed = (total[:, cols] / columns[:, h : h + 1]).astype(jnp.bfloat16)
        upper_ref[:, cols] = normed[:half]
        lower_ref[:, cols] = normed[half:]


def finish(own, sums, got):
    rows, width = own.shape
    vmem = pl.BlockSpec(memory_space=pltpu.VMEM)
    half = jax.ShapeDtypeStruct((rows // 2, width), jnp.bfloat16)
    return pl.pallas_call(
        finish_kernel,
        in_specs=[vmem] * 3,
        out_specs=[vmem] * 2,
        out_shape=[half, half],
        compiler_params=pltpu.CompilerParams(vmem_limit_bytes=8 * MIB),
        name="finish",
    )(own, sums, got)


def arrange_kernel(place_ref, own_ref, mate_ref, out_ref):
    c = place_ref[8]
    y_lo, z, core = c // 16, lax.rem(c // 2, N_Z), lax.rem(c, 2)
    for r in range(8):
        distance = lax.rem(place_ref[r] - z + N_Z, N_Z)
        slot = 0
        for d, held in enumerate(RING_SLOT):
            slot = jnp.where(distance == d, held, slot)
        for n in range(4):
            held, far = (own_ref, mate_ref)[n // 2], n % 2
            part = lax.rem(core + n // 2, 2) * 2 + lax.rem(y_lo + far, 2)
            out_ref[r, part] = held[far * 8 + slot]


def arrange_weight(own, mate, places):
    _, cols, width = own.shape
    vmem = pl.BlockSpec(memory_space=pltpu.VMEM)
    return pl.pallas_call(
        arrange_kernel,
        in_specs=[pl.BlockSpec(memory_space=pltpu.SMEM)] + [vmem] * 2,
        out_specs=vmem,
        out_shape=jax.ShapeDtypeStruct((8, 4, cols, width), own.dtype),
        compiler_params=pltpu.CompilerParams(vmem_limit_bytes=16 * MIB),
        cost_estimate=pl.CostEstimate(flops=0, bytes_accessed=8 * MIB, transcendentals=0),
        name="arrange",
    )(places, own, mate)


HERE, THERE = (0, 1, 2, 3), (4, 5, 6, 7)


def term_of(rows, w_ref, r):
    weight = w_ref[r].reshape(-1, rows.shape[1])
    return lax.dot_general(rows, weight, (((1,), (1,)), ((), ())), preferred_element_type=jnp.float32)


def project_kernel(b0, b1, b2, b3, along, w_ref, upper_ref, lower_ref):
    half = upper_ref.shape[0]
    upper = lower = None
    for n, both in enumerate((b0, b1, b2, b3)):
        for rows, r in ((both[:half], HERE[n]), (both[half:], THERE[n])):
            term = term_of(rows, w_ref, r)
            upper = term if upper is None else upper + term
        term = term_of(along[n * half : (n + 1) * half], w_ref, HERE[n])
        lower = term if lower is None else lower + term
    upper_ref[...] = upper.astype(jnp.bfloat16)
    lower_ref[...] = lower


def project_last_kernel(upper_ref, lower_ref, far, w_ref, out_ref):
    half = upper_ref.shape[0]
    out_ref[:half] = upper_ref[...]
    lower = lower_ref[...]
    for n in range(4):
        lower = lower + term_of(far[n * half : (n + 1) * half], w_ref, THERE[n])
    out_ref[half:] = lower.astype(jnp.bfloat16)


def project(both, along, far, weight):
    rows, width = both[0].shape
    half = rows // 2
    columns = weight.shape[1] * weight.shape[2]
    vmem = pl.BlockSpec(memory_space=pltpu.VMEM)

    def call(kernel, args, out_shape, terms):
        return pl.pallas_call(
            kernel,
            in_specs=[vmem] * len(args),
            out_specs=[vmem] * len(out_shape),
            out_shape=out_shape,
            compiler_params=pltpu.CompilerParams(vmem_limit_bytes=16 * MIB),
            cost_estimate=pl.CostEstimate(
                flops=2 * half * terms * width * columns, bytes_accessed=8 * width * columns * 2, transcendentals=0
            ),
            name="project",
        )(*args)

    upper, lower = call(
        project_kernel,
        [*both, along, weight],
        [
            jax.ShapeDtypeStruct((half, columns), jnp.bfloat16),
            jax.ShapeDtypeStruct((half, columns), jnp.float32),
        ],
        12,
    )
    return call(
        project_last_kernel,
        [upper, lower, far, weight],
        [jax.ShapeDtypeStruct((rows, columns), jnp.bfloat16)],
        4,
    )[0]


RING_SLOT = (0, 2, 4, 6, 7, 5, 3, 1)


def regroup_weight(out_weight):
    pairs = []
    for c in range(N_CTX):
        c_lo, c_z, c_core = c // 16, (c // 2) % N_Z, c % 2
        for t in range(N_TP):
            pairs.append(((4 * t + c_core * 2 + c_lo) * N_TP + c_z, c * N_TP + t))
    return lax.ppermute(out_weight.T, ("ctx", "tp"), pairs)


def on_device(tokens, qkv_weight, query_gain, key_gain, out_weight, block_ids):
    places = sender_places()
    out_block = regroup_weight(out_weight)
    half = tokens.shape[0] // 2
    weight = order_weight(qkv_weight.transpose(1, 0, 2), places)
    q_flat, k_flat, values, squares = qkv(
        *gather_tp(tokens[:half], tokens[half:]), weight, out_block
    )

    pair_sum = squares + move(squares, y_hi=1)
    tied = after(values, pair_sum)
    v_up, v_down = [values, move(tied, z=1)], [values, move(tied, z=-1)]
    parts = [pair_sum] + [move(pair_sum, x=x) for x in (2, 1, 3)]
    queries, keys = norm(
        block_ids, parts, after(q_flat, v_up[1], v_down[1]), k_flat, query_gain.reshape(1, -1), key_gain.reshape(1, -1)
    )

    k_up, k_down = [keys, move(keys, z=1)], [keys, move(keys, z=-1)]
    across = move(queries, y_lo=1)
    mate = move(after(queries, k_up[1]), core=1)
    qs = [queries, mate, across, move(across, core=1)]

    rows = block_ids.shape[0]
    for _ in range(2):
        v_up.append(move(v_up[-1], z=1))
        v_down.append(move(v_down[-1], z=-1))
    v_far = move(v_down[3], z=-1)
    first = jnp.stack([v[rows:] for v in (values, v_up[1], v_down[1])])
    middle = jnp.stack([v[rows:] for v in (v_up[2], v_down[2], v_up[3], v_down[3])])
    first_far, middle_far = move(after(first, across, k_up[1], k_down[1]), y_lo=1), move(middle, y_lo=1)

    k_up.append(move(k_up[1], z=1))
    k_down.append(move(k_down[1], z=-1))
    (state,) = attend(qs, [keys, k_up[1], k_down[1]], [values, v_up[1], v_down[1]], None, False)
    k_up.append(move(after(k_up[2], state), z=1))
    k_down.append(move(after(k_down[2], state), z=-1))
    (state,) = attend(qs, [k_up[2], k_down[2]], [v_up[2], v_down[2]], state, False)
    k_far = move(after(k_up[3], state), z=1)
    (state,) = attend(qs, [k_up[3], k_down[3]], [v_up[3], v_down[3]], state, False)
    keep, sums, send = attend(qs, [k_far], [v_far], state, True)

    own, sums, send = fold(keep, sums, move(send, core=1))
    got = move(send, y_lo=1)
    late = v_far[None, rows:]
    out_own = jnp.concatenate([first, middle, late, first_far, middle_far, move(late, y_lo=1)])
    out_mate = move(after(out_own, got), core=1)
    upper, lower = finish(own, sums, got)
    both, along, far = gather_tp(upper, lower)
    out_whole = arrange_weight(out_own, out_mate, places)
    return project(both, along, far, out_whole)


def solution(mesh):
    in_specs = (P("ctx", "tp"), P(None, None, "tp"), P("tp"), P("tp"), P("tp", "ctx"), P("ctx"))
    out_specs = P("ctx", "tp")
    return jax.shard_map(
        on_device, mesh=mesh, in_specs=in_specs, out_specs=out_specs, check_vma=False
    )
```

```python
import math

import jax
import jax.numpy as jnp
from jax import lax
from jax.experimental import pallas as pl
from jax.experimental.pallas import tpu as pltpu
from jax.sharding import PartitionSpec as P

HEADS = 24
HD = 128
ID_ROWS = 16
N_Z = 8
N_X = 4
N_TP = 8
N_CTX = 32
MIB = 1 << 20


def move(value, x=0, y_hi=0, y_lo=0, z=0, core=0):
    pairs = []
    for c in range(N_CTX):
        for t in range(N_TP):
            c_lo, c_z, c_core = c // 16, (c // 2) % 8, c % 2
            t_x, t_hi = t // 2, t % 2
            dst_c = ((c_lo + y_lo) % 2) * 16 + ((c_z + z) % N_Z) * 2 + (c_core + core) % 2
            dst_t = ((t_x + x) % N_X) * 2 + (t_hi + y_hi) % 2
            pairs.append((c * N_TP + t, dst_c * N_TP + dst_t))
    return lax.ppermute(value, ("ctx", "tp"), pairs)


TP_STEPS = [(0, 0), (1, 0), (3, 0), (2, 0), (0, 1), (1, 1), (3, 1), (2, 1)]


def after(value, *others):
    return lax.optimization_barrier((value, *others))[0]


def gather_tp(upper, lower):
    both = jnp.concatenate([upper, move(upper, y_hi=1)])
    along = jnp.concatenate([lower] + [move(lower, x=x) for x in (1, 3, 2)])
    far = move(along, y_hi=1)
    return [both] + [move(both, x=x) for x in (1, 3, 2)], along, far


def sender_places():
    t = lax.axis_index("tp")
    t_x, t_hi = t // 2, t % 2
    places = [((t_x - x + N_X) % N_X) * 2 + (t_hi - y_hi + 2) % 2 for x, y_hi in TP_STEPS]
    return jnp.stack(places + [lax.axis_index("ctx")]).astype(jnp.int32)


def order_kernel(place_ref, w_ref, out_ref, sems):
    feats = out_ref.shape[1] // 8

    def fetch(r):
        start = pl.multiple_of(place_ref[r] * feats, feats)
        return pltpu.make_async_copy(
            w_ref.at[:, pl.ds(start, feats), :], out_ref.at[:, pl.ds(r * feats, feats), :], sems.at[r]
        )

    for r in range(8):
        fetch(r).start()
    for r in range(8):
        fetch(r).wait()


def order_weight(weight, places):
    return pl.pallas_call(
        order_kernel,
        in_specs=[pl.BlockSpec(memory_space=pltpu.SMEM), pl.BlockSpec(memory_space=pl.ANY)],
        out_specs=pl.BlockSpec(memory_space=pltpu.VMEM),
        out_shape=jax.ShapeDtypeStruct(weight.shape, weight.dtype),
        scratch_shapes=[pltpu.SemaphoreType.DMA((8,))],
        compiler_params=pltpu.CompilerParams(vmem_limit_bytes=32 * MIB),
        cost_estimate=pl.CostEstimate(flops=0, bytes_accessed=24 * MIB, transcendentals=0),
        name="order",
    )(places, weight)


def product(rows, w_ref, p, block):
    wide = jnp.concatenate(rows, axis=1) if len(rows) > 1 else rows[0]
    feats = w_ref.shape[1] // 8
    return jnp.dot(
        wide, w_ref[p, block * feats : block * feats + wide.shape[1], :], preferred_element_type=jnp.float32
    )


def lower_kernel(block, *refs):
    held, w_ref, out_ref = refs[0], refs[-2], refs[-1]
    half = held.shape[0] // 4
    rows = [held[n * half : (n + 1) * half] for n in range(4)]
    for p in range(3):
        term = product(rows, w_ref, p, block)
        out_ref[p] = term if block == 0 else refs[1][p] + term


def upper_kernel(b0, b1, b2, w_ref, out_ref):
    half = b0.shape[0] // 2
    for p in range(3):
        here = product([b[:half] for b in (b0, b1, b2)], w_ref, p, 0)
        out_ref[p] = here + product([b[half:] for b in (b0, b1, b2)], w_ref, p, 4)


def last_kernel(b3, upper_ref, lower_ref, w_ref, out_w, q_ref, k_ref, v_ref, sq_ref):
    half = b3.shape[0] // 2

    def whole(p):
        upper = upper_ref[p] + product([b3[:half]], w_ref, p, 3) + product([b3[half:]], w_ref, p, 7)
        return jnp.concatenate([upper, lower_ref[p]], axis=0)

    q, k, v = [whole(p) for p in range(3)]
    q_ref[...] = q
    k_ref[...] = k
    v_ref[: v.shape[0]] = v.astype(jnp.bfloat16)
    v_ref[v.shape[0] :] = out_w[...]
    q_sq = jnp.sum(q * q, axis=1, keepdims=True)
    k_sq = jnp.sum(k * k, axis=1, keepdims=True)
    lane = lax.broadcasted_iota(jnp.int32, (q.shape[0], 128), 1)
    both = jnp.where(lane == 0, q_sq, jnp.where(lane == 1, k_sq, 0.0))
    sq_ref[...] = both.T[:8]


def qkv(firsts, along, far, weight, out_block):
    rows, feats = firsts[0].shape
    half = rows // 2
    width = weight.shape[2]
    vmem = pl.BlockSpec(memory_space=pltpu.VMEM)
    share = jax.ShapeDtypeStruct((3, half, width), jnp.float32)

    def call(kernel, args, out_shape, blocks):
        return pl.pallas_call(
            kernel,
            in_specs=[vmem] * len(args),
            out_specs=[vmem] * len(out_shape),
            out_shape=out_shape,
            compiler_params=pltpu.CompilerParams(vmem_limit_bytes=32 * MIB),
            cost_estimate=pl.CostEstimate(
                flops=2 * half * blocks * feats * 3 * width,
                bytes_accessed=blocks * feats * 3 * width * 2,
                transcendentals=0,
            ),
            name="qkv",
        )(*args)

    def lower_part(block, *args):
        return call(lambda *refs: lower_kernel(block, *refs), [*args, weight], [share], 4)[0]

    lower = lower_part(0, along)
    lower = lower_part(4, far, lower)
    (upper,) = call(upper_kernel, [*firsts[:3], weight], [share], 6)
    whole = jax.ShapeDtypeStruct((rows, width), jnp.float32)
    return call(
        last_kernel,
        [firsts[3], upper, lower, weight, out_block],
        [
            whole,
            whole,
            jax.ShapeDtypeStruct((rows + out_block.shape[0], width), jnp.bfloat16),
            jax.ShapeDtypeStruct((8, rows), jnp.float32),
        ],
        2,
    )


def norm_kernel(id_ref, s0, s1, s2, s3, q_ref, k_ref, qg_ref, kg_ref, q_out, k_out):
    rows = q_ref.shape[0]
    total = s0[...] + s1[...] + s2[...] + s3[...]
    inverse = lax.rsqrt(total * (1.0 / (HEADS * HD)) + 1e-06)
    columns = jnp.concatenate([inverse, jnp.zeros((120, rows), jnp.float32)], axis=0).T
    q_scale = math.log2(math.e) / math.sqrt(HD)
    q_out[:rows] = (q_ref[...] * columns[:, 0:1] * (qg_ref[...] * q_scale)).astype(jnp.bfloat16)
    k_out[:rows] = (k_ref[...] * columns[:, 1:2] * kg_ref[...]).astype(jnp.bfloat16)
    span = jnp.full((ID_ROWS, q_ref.shape[1]), id_ref[0].astype(jnp.float32), jnp.float32)
    q_out[rows:] = span.astype(jnp.bfloat16)
    k_out[rows:] = span.astype(jnp.bfloat16)


def norm(span_id, squares, q, k, q_gain, k_gain):
    rows, width = q.shape
    vmem = pl.BlockSpec(memory_space=pltpu.VMEM)
    out = jax.ShapeDtypeStruct((rows + ID_ROWS, width), jnp.bfloat16)
    return pl.pallas_call(
        norm_kernel,
        in_specs=[pl.BlockSpec(memory_space=pltpu.SMEM)] + [vmem] * 8,
        out_specs=[vmem] * 2,
        out_shape=[out, out],
        compiler_params=pltpu.CompilerParams(vmem_limit_bytes=12 * MIB),
        name="norm",
    )(span_id, *squares, q, k, q_gain, k_gain)


def attend_kernel(n_keys, first, last, *refs):
    qs, ks, vs = refs[:4], refs[4 : 4 + n_keys], refs[4 + n_keys : 4 + 2 * n_keys]
    rest = refs[4 + 2 * n_keys :]
    rows = qs[0].shape[0] - ID_ROWS
    heads = vs[0].shape[1] // HD
    if first:
        acc_ref, = rest[:1]
        acc_ref[...] = jnp.zeros_like(acc_ref)
    elif last:
        acc_in, keep_ref, keep_sum, send_ref, acc_ref = rest
        acc_ref[...] = acc_in[...]
    else:
        acc_in, acc_ref = rest
        acc_ref[...] = acc_in[...]
    lane = lax.broadcasted_iota(jnp.int32, (rows, HD), 1)
    ones = jnp.ones((rows, HD), jnp.bfloat16)
    q_ids = [jnp.max(q[rows:, :HD].astype(jnp.float32)) for q in qs]
    k_ids = [jnp.max(k[rows:, :HD].astype(jnp.float32)) for k in ks]
    for i in range(4):
        for j in range(n_keys):

            @pl.when(k_ids[j] <= q_ids[i])
            def _():
                sums = None
                for h in range(heads):
                    cols = slice(h * HD, (h + 1) * HD)
                    scores = lax.dot_general(
                        qs[i][:rows, cols], ks[j][:rows, cols], (((1,), (1,)), ((), ())),
                        preferred_element_type=jnp.float32,
                    )
                    weights = jnp.exp2(scores).astype(jnp.bfloat16)
                    wide = jnp.concatenate([vs[j][:rows, cols], ones], axis=1)
                    both = jnp.dot(weights, wide, preferred_element_type=jnp.float32)
                    acc_ref[i, :, cols] += both[:, :HD]
                    sums = both[:, HD:] if h == 0 else jnp.where(lane == h, both[:, HD:], sums)
                acc_ref[i, :, heads * HD :] += sums
    if last:
        for n, i in enumerate((0, 2)):
            keep_ref[n] = acc_ref[i, :, : heads * HD]
            keep_sum[n] = acc_ref[i, :, heads * HD :].T[:8]
        for n, i in enumerate((1, 3)):
            write_share(send_ref.at[n], acc_ref[i, :, : heads * HD], acc_ref[i, :, heads * HD :].T[:8])


def write_share(ref, sums, totals):
    rows = sums.shape[0]
    ref[:rows] = sums.astype(jnp.bfloat16)
    pad = jnp.zeros((8, sums.shape[1] - rows), jnp.float32)
    high = totals.astype(jnp.bfloat16).astype(jnp.float32)
    low = totals - high
    both = jnp.concatenate(
        [jnp.concatenate([high, pad], axis=1), jnp.concatenate([low, pad], axis=1)], axis=0
    )
    ref[rows:] = both.astype(jnp.bfloat16)


def read_totals(ref, rows):
    both = ref[rows:, :rows].astype(jnp.float32)
    return both[:8] + both[8:]


def attend(qs, ks, vs, state, last):
    rows, width = qs[0].shape[0] - ID_ROWS, vs[0].shape[1]
    n_keys = len(ks)
    wide = width + HD
    vmem = pl.BlockSpec(memory_space=pltpu.VMEM)
    state_shape = jax.ShapeDtypeStruct((4, rows, wide), jnp.float32)
    if last:
        out_shape = [
            jax.ShapeDtypeStruct((2, rows, width), jnp.float32),
            jax.ShapeDtypeStruct((2, 8, rows), jnp.float32),
            jax.ShapeDtypeStruct((2, rows + ID_ROWS, width), jnp.bfloat16),
        ]
        scratch = [pltpu.VMEM((4, rows, wide), jnp.float32)]
    else:
        out_shape, scratch = [state_shape], []
    first = state is None
    args = [*qs, *ks, *vs] + ([] if first else [state])

    def body(*refs):
        attend_kernel(n_keys, first, last, *refs)

    flops = 4 * n_keys * 3 * rows * rows * HD * 4
    return pl.pallas_call(
        body,
        in_specs=[vmem] * len(args),
        out_specs=[vmem] * len(out_shape),
        out_shape=out_shape,
        scratch_shapes=scratch,
        compiler_params=pltpu.CompilerParams(vmem_limit_bytes=32 * MIB),
        cost_estimate=pl.CostEstimate(
            flops=flops, bytes_accessed=8 * MIB, transcendentals=4 * n_keys * 3 * rows * rows
        ),
        name="attend",
    )(*args)


def fold_kernel(keep_ref, sum_ref, got_ref, own_ref, own_sum, send_ref):
    rows = keep_ref.shape[1]
    own_ref[...] = keep_ref[0] + got_ref[0, :rows].astype(jnp.float32)
    own_sum[...] = sum_ref[0] + read_totals(got_ref.at[0], rows)
    write_share(
        send_ref,
        keep_ref[1] + got_ref[1, :rows].astype(jnp.float32),
        sum_ref[1] + read_totals(got_ref.at[1], rows),
    )


def fold(keep, sums, got):
    _, rows, width = keep.shape
    vmem = pl.BlockSpec(memory_space=pltpu.VMEM)
    return pl.pallas_call(
        fold_kernel,
        in_specs=[vmem] * 3,
        out_specs=[vmem] * 3,
        out_shape=[
            jax.ShapeDtypeStruct((rows, width), jnp.float32),
            jax.ShapeDtypeStruct((8, rows), jnp.float32),
            jax.ShapeDtypeStruct((rows + ID_ROWS, width), jnp.bfloat16),
        ],
        compiler_params=pltpu.CompilerParams(vmem_limit_bytes=8 * MIB),
        name="fold",
    )(keep, sums, got)


def finish_kernel(own_ref, sum_ref, got_ref, upper_ref, lower_ref):
    half, width = upper_ref.shape
    rows = 2 * half
    total = own_ref[...] + got_ref[:rows].astype(jnp.float32)
    sums = sum_ref[...] + read_totals(got_ref, rows)
    columns = jnp.concatenate([sums, jnp.ones((120, rows), jnp.float32)], axis=0).T
    for h in range(width // HD):
        cols = slice(h * HD, (h + 1) * HD)
        normed = (total[:, cols] / columns[:, h : h + 1]).astype(jnp.bfloat16)
        upper_ref[:, cols] = normed[:half]
        lower_ref[:, cols] = normed[half:]


def finish(own, sums, got):
    rows, width = own.shape
    vmem = pl.BlockSpec(memory_space=pltpu.VMEM)
    half = jax.ShapeDtypeStruct((rows // 2, width), jnp.bfloat16)
    return pl.pallas_call(
        finish_kernel,
        in_specs=[vmem] * 3,
        out_specs=[vmem] * 2,
        out_shape=[half, half],
        compiler_params=pltpu.CompilerParams(vmem_limit_bytes=8 * MIB),
        name="finish",
    )(own, sums, got)


def arrange_kernel(place_ref, own_ref, mate_ref, out_ref):
    c = place_ref[8]
    y_lo, z, core = c // 16, lax.rem(c // 2, N_Z), lax.rem(c, 2)
    for r in range(8):
        distance = lax.rem(place_ref[r] - z + N_Z, N_Z)
        slot = 0
        for d, held in enumerate(RING_SLOT):
            slot = jnp.where(distance == d, held, slot)
        for n in range(4):
            held, far = (own_ref, mate_ref)[n // 2], n % 2
            part = lax.rem(core + n // 2, 2) * 2 + lax.rem(y_lo + far, 2)
            out_ref[r, part] = held[far * 8 + slot]


def arrange_weight(own, mate, places):
    _, cols, width = own.shape
    vmem = pl.BlockSpec(memory_space=pltpu.VMEM)
    return pl.pallas_call(
        arrange_kernel,
        in_specs=[pl.BlockSpec(memory_space=pltpu.SMEM)] + [vmem] * 2,
        out_specs=vmem,
        out_shape=jax.ShapeDtypeStruct((8, 4, cols, width), own.dtype),
        compiler_params=pltpu.CompilerParams(vmem_limit_bytes=16 * MIB),
        cost_estimate=pl.CostEstimate(flops=0, bytes_accessed=8 * MIB, transcendentals=0),
        name="arrange",
    )(places, own, mate)


HERE, THERE = (0, 1, 2, 3), (4, 5, 6, 7)


def term_of(rows, w_ref, r):
    weight = w_ref[r].reshape(-1, rows.shape[1])
    return lax.dot_general(rows, weight, (((1,), (1,)), ((), ())), preferred_element_type=jnp.float32)


def project_kernel(b0, b1, b2, b3, along, w_ref, upper_ref, lower_ref):
    half = upper_ref.shape[0]
    upper = lower = None
    for n, both in enumerate((b0, b1, b2, b3)):
        for rows, r in ((both[:half], HERE[n]), (both[half:], THERE[n])):
            term = term_of(rows, w_ref, r)
            upper = term if upper is None else upper + term
        term = term_of(along[n * half : (n + 1) * half], w_ref, HERE[n])
        lower = term if lower is None else lower + term
    upper_ref[...] = upper.astype(jnp.bfloat16)
    lower_ref[...] = lower


def project_last_kernel(upper_ref, lower_ref, far, w_ref, out_ref):
    half = upper_ref.shape[0]
    out_ref[:half] = upper_ref[...]
    lower = lower_ref[...]
    for n in range(4):
        lower = lower + term_of(far[n * half : (n + 1) * half], w_ref, THERE[n])
    out_ref[half:] = lower.astype(jnp.bfloat16)


def project(both, along, far, weight):
    rows, width = both[0].shape
    half = rows // 2
    columns = weight.shape[1] * weight.shape[2]
    vmem = pl.BlockSpec(memory_space=pltpu.VMEM)

    def call(kernel, args, out_shape, terms):
        return pl.pallas_call(
            kernel,
            in_specs=[vmem] * len(args),
            out_specs=[vmem] * len(out_shape),
            out_shape=out_shape,
            compiler_params=pltpu.CompilerParams(vmem_limit_bytes=16 * MIB),
            cost_estimate=pl.CostEstimate(
                flops=2 * half * terms * width * columns, bytes_accessed=8 * width * columns * 2, transcendentals=0
            ),
            name="project",
        )(*args)

    upper, lower = call(
        project_kernel,
        [*both, along, weight],
        [
            jax.ShapeDtypeStruct((half, columns), jnp.bfloat16),
            jax.ShapeDtypeStruct((half, columns), jnp.float32),
        ],
        12,
    )
    return call(
        project_last_kernel,
        [upper, lower, far, weight],
        [jax.ShapeDtypeStruct((rows, columns), jnp.bfloat16)],
        4,
    )[0]


RING_SLOT = (0, 2, 4, 6, 7, 5, 3, 1)


def regroup_weight(out_weight):
    pairs = []
    for c in range(N_CTX):
        c_lo, c_z, c_core = c // 16, (c // 2) % N_Z, c % 2
        for t in range(N_TP):
            pairs.append(((4 * t + c_core * 2 + c_lo) * N_TP + c_z, c * N_TP + t))
    return lax.ppermute(out_weight.T, ("ctx", "tp"), pairs)


def on_device(tokens, qkv_weight, query_gain, key_gain, out_weight, block_ids):
    places = sender_places()
    out_block = regroup_weight(out_weight)
    half = tokens.shape[0] // 2
    weight = order_weight(qkv_weight.transpose(1, 0, 2), places)
    q_flat, k_flat, values, squares = qkv(
        *gather_tp(tokens[:half], tokens[half:]), weight, out_block
    )

    pair_sum = squares + move(squares, y_hi=1)
    parts = [pair_sum] + [move(pair_sum, x=x) for x in (2, 1, 3)]
    tied = after(values, parts[1])
    v_up, v_down = [values, move(tied, z=1)], [values, move(tied, z=-1)]
    queries, keys = norm(
        block_ids, parts, q_flat, k_flat, query_gain.reshape(1, -1), key_gain.reshape(1, -1)
    )

    k_up, k_down = [keys, move(keys, z=1)], [keys, move(keys, z=-1)]
    across = move(queries, y_lo=1)
    mate = move(after(queries, k_up[1]), core=1)
    qs = [queries, mate, across, move(across, core=1)]

    rows = block_ids.shape[0]
    for _ in range(2):
        v_up.append(move(v_up[-1], z=1))
        v_down.append(move(v_down[-1], z=-1))
    v_far = move(v_down[3], z=-1)
    first = jnp.stack([v[rows:] for v in (values, v_up[1], v_down[1])])
    middle = jnp.stack([v[rows:] for v in (v_up[2], v_down[2], v_up[3], v_down[3])])
    first_far, middle_far = move(after(first, across, v_up[2], v_down[2]), y_lo=1), move(middle, y_lo=1)

    k_up.append(move(after(k_up[1], v_up[1], v_down[1]), z=1))
    k_down.append(move(after(k_down[1], v_up[1], v_down[1]), z=-1))
    (state,) = attend(qs, [keys, k_up[1], k_down[1]], [values, v_up[1], v_down[1]], None, False)
    k_up.append(move(after(k_up[2], state), z=1))
    k_down.append(move(after(k_down[2], state), z=-1))
    (state,) = attend(qs, [k_up[2], k_down[2]], [v_up[2], v_down[2]], state, False)
    k_far = move(after(k_up[3], state), z=1)
    (state,) = attend(qs, [k_up[3], k_down[3]], [v_up[3], v_down[3]], state, False)
    keep, sums, send = attend(qs, [k_far], [v_far], state, True)

    own, sums, send = fold(keep, sums, move(send, core=1))
    got = move(send, y_lo=1)
    late = v_far[None, rows:]
    out_own = jnp.concatenate([first, middle, late, first_far, middle_far, move(late, y_lo=1)])
    out_mate = move(after(out_own, got), core=1)
    upper, lower = finish(own, sums, got)
    both, along, far = gather_tp(upper, lower)
    out_whole = arrange_weight(out_own, out_mate, places)
    return project(both, along, far, out_whole)


def solution(mesh):
    in_specs = (P("ctx", "tp"), P(None, None, "tp"), P("tp"), P("tp"), P("tp", "ctx"), P("ctx"))
    out_specs = P("ctx", "tp")
    return jax.shard_map(
        on_device, mesh=mesh, in_specs=in_specs, out_specs=out_specs, check_vma=False
    )
```

```python
import math

import jax
import jax.numpy as jnp
from jax import lax
from jax.experimental import pallas as pl
from jax.experimental.pallas import tpu as pltpu
from jax.sharding import PartitionSpec as P

HEADS = 24
HD = 128
ID_ROWS = 16
N_Z = 8
N_X = 4
N_TP = 8
N_CTX = 32
MIB = 1 << 20


def move(value, x=0, y_hi=0, y_lo=0, z=0, core=0):
    pairs = []
    for c in range(N_CTX):
        for t in range(N_TP):
            c_lo, c_z, c_core = c // 16, (c // 2) % 8, c % 2
            t_x, t_hi = t // 2, t % 2
            dst_c = ((c_lo + y_lo) % 2) * 16 + ((c_z + z) % N_Z) * 2 + (c_core + core) % 2
            dst_t = ((t_x + x) % N_X) * 2 + (t_hi + y_hi) % 2
            pairs.append((c * N_TP + t, dst_c * N_TP + dst_t))
    return lax.ppermute(value, ("ctx", "tp"), pairs)


TP_STEPS = [(0, 0), (1, 0), (3, 0), (2, 0), (0, 1), (1, 1), (3, 1), (2, 1)]


def after(value, *others):
    return lax.optimization_barrier((value, *others))[0]


def gather_tp(upper, lower):
    both = jnp.concatenate([upper, move(upper, y_hi=1)])
    along = jnp.concatenate([lower] + [move(lower, x=x) for x in (1, 3, 2)])
    far = move(along, y_hi=1)
    return [both] + [move(both, x=x) for x in (1, 3, 2)], along, far


def sender_places():
    t = lax.axis_index("tp")
    t_x, t_hi = t // 2, t % 2
    places = [((t_x - x + N_X) % N_X) * 2 + (t_hi - y_hi + 2) % 2 for x, y_hi in TP_STEPS]
    return jnp.stack(places + [lax.axis_index("ctx")]).astype(jnp.int32)


def order_kernel(place_ref, w_ref, out_ref, sems):
    feats = out_ref.shape[1] // 8

    def fetch(r):
        start = pl.multiple_of(place_ref[r] * feats, feats)
        return pltpu.make_async_copy(
            w_ref.at[:, pl.ds(start, feats), :], out_ref.at[:, pl.ds(r * feats, feats), :], sems.at[r]
        )

    for r in range(8):
        fetch(r).start()
    for r in range(8):
        fetch(r).wait()


def order_weight(weight, places):
    return pl.pallas_call(
        order_kernel,
        in_specs=[pl.BlockSpec(memory_space=pltpu.SMEM), pl.BlockSpec(memory_space=pl.ANY)],
        out_specs=pl.BlockSpec(memory_space=pltpu.VMEM),
        out_shape=jax.ShapeDtypeStruct(weight.shape, weight.dtype),
        scratch_shapes=[pltpu.SemaphoreType.DMA((8,))],
        compiler_params=pltpu.CompilerParams(vmem_limit_bytes=32 * MIB),
        cost_estimate=pl.CostEstimate(flops=0, bytes_accessed=24 * MIB, transcendentals=0),
        name="order",
    )(places, weight)


def product(rows, w_ref, p, block):
    wide = jnp.concatenate(rows, axis=1) if len(rows) > 1 else rows[0]
    feats = w_ref.shape[1] // 8
    return jnp.dot(
        wide, w_ref[p, block * feats : block * feats + wide.shape[1], :], preferred_element_type=jnp.float32
    )


def lower_kernel(block, *refs):
    held, w_ref, out_ref = refs[0], refs[-2], refs[-1]
    half = held.shape[0] // 4
    rows = [held[n * half : (n + 1) * half] for n in range(4)]
    for p in range(3):
        term = product(rows, w_ref, p, block)
        out_ref[p] = term if block == 0 else refs[1][p] + term


def upper_kernel(b0, b1, b2, w_ref, out_ref):
    half = b0.shape[0] // 2
    for p in range(3):
        here = product([b[:half] for b in (b0, b1, b2)], w_ref, p, 0)
        out_ref[p] = here + product([b[half:] for b in (b0, b1, b2)], w_ref, p, 4)


def last_kernel(b3, upper_ref, lower_ref, w_ref, out_w, q_ref, k_ref, v_ref, sq_ref):
    half = b3.shape[0] // 2

    def whole(p):
        upper = upper_ref[p] + product([b3[:half]], w_ref, p, 3) + product([b3[half:]], w_ref, p, 7)
        return jnp.concatenate([upper, lower_ref[p]], axis=0)

    q, k, v = [whole(p) for p in range(3)]
    q_ref[...] = q
    k_ref[...] = k
    v_ref[: v.shape[0]] = v.astype(jnp.bfloat16)
    v_ref[v.shape[0] :] = out_w[...]
    q_sq = jnp.sum(q * q, axis=1, keepdims=True)
    k_sq = jnp.sum(k * k, axis=1, keepdims=True)
    lane = lax.broadcasted_iota(jnp.int32, (q.shape[0], 128), 1)
    both = jnp.where(lane == 0, q_sq, jnp.where(lane == 1, k_sq, 0.0))
    sq_ref[...] = both.T[:8]


def qkv(firsts, along, far, weight, out_block):
    rows, feats = firsts[0].shape
    half = rows // 2
    width = weight.shape[2]
    vmem = pl.BlockSpec(memory_space=pltpu.VMEM)
    share = jax.ShapeDtypeStruct((3, half, width), jnp.float32)

    def call(kernel, args, out_shape, blocks):
        return pl.pallas_call(
            kernel,
            in_specs=[vmem] * len(args),
            out_specs=[vmem] * len(out_shape),
            out_shape=out_shape,
            compiler_params=pltpu.CompilerParams(vmem_limit_bytes=32 * MIB),
            cost_estimate=pl.CostEstimate(
                flops=2 * half * blocks * feats * 3 * width,
                bytes_accessed=blocks * feats * 3 * width * 2,
                transcendentals=0,
            ),
            name="qkv",
        )(*args)

    def lower_part(block, *args):
        return call(lambda *refs: lower_kernel(block, *refs), [*args, weight], [share], 4)[0]

    lower = lower_part(0, along)
    lower = lower_part(4, far, lower)
    (upper,) = call(upper_kernel, [*firsts[:3], weight], [share], 6)
    whole = jax.ShapeDtypeStruct((rows, width), jnp.float32)
    return call(
        last_kernel,
        [firsts[3], upper, lower, weight, out_block],
        [
            whole,
            whole,
            jax.ShapeDtypeStruct((rows + out_block.shape[0], width), jnp.bfloat16),
            jax.ShapeDtypeStruct((8, rows), jnp.float32),
        ],
        2,
    )


def norm_kernel(id_ref, s0, s1, s2, s3, q_ref, k_ref, qg_ref, kg_ref, q_out, k_out):
    rows = q_ref.shape[0]
    total = s0[...] + s1[...] + s2[...] + s3[...]
    inverse = lax.rsqrt(total * (1.0 / (HEADS * HD)) + 1e-06)
    columns = jnp.concatenate([inverse, jnp.zeros((120, rows), jnp.float32)], axis=0).T
    q_scale = math.log2(math.e) / math.sqrt(HD)
    q_out[:rows] = (q_ref[...] * columns[:, 0:1] * (qg_ref[...] * q_scale)).astype(jnp.bfloat16)
    k_out[:rows] = (k_ref[...] * columns[:, 1:2] * kg_ref[...]).astype(jnp.bfloat16)
    span = jnp.full((ID_ROWS, q_ref.shape[1]), id_ref[0].astype(jnp.float32), jnp.float32)
    q_out[rows:] = span.astype(jnp.bfloat16)
    k_out[rows:] = span.astype(jnp.bfloat16)


def norm(span_id, squares, q, k, q_gain, k_gain):
    rows, width = q.shape
    vmem = pl.BlockSpec(memory_space=pltpu.VMEM)
    out = jax.ShapeDtypeStruct((rows + ID_ROWS, width), jnp.bfloat16)
    return pl.pallas_call(
        norm_kernel,
        in_specs=[pl.BlockSpec(memory_space=pltpu.SMEM)] + [vmem] * 8,
        out_specs=[vmem] * 2,
        out_shape=[out, out],
        compiler_params=pltpu.CompilerParams(vmem_limit_bytes=12 * MIB),
        name="norm",
    )(span_id, *squares, q, k, q_gain, k_gain)


def attend_kernel(n_keys, first, last, *refs):
    qs, ks, vs = refs[:4], refs[4 : 4 + n_keys], refs[4 + n_keys : 4 + 2 * n_keys]
    rest = refs[4 + 2 * n_keys :]
    rows = qs[0].shape[0] - ID_ROWS
    heads = vs[0].shape[1] // HD
    if first:
        acc_ref, = rest[:1]
        acc_ref[...] = jnp.zeros_like(acc_ref)
    elif last:
        acc_in, keep_ref, keep_sum, send_ref, acc_ref = rest
        acc_ref[...] = acc_in[...]
    else:
        acc_in, acc_ref = rest
        acc_ref[...] = acc_in[...]
    lane = lax.broadcasted_iota(jnp.int32, (rows, HD), 1)
    ones = jnp.ones((rows, HD), jnp.bfloat16)
    q_ids = [jnp.max(q[rows:, :HD].astype(jnp.float32)) for q in qs]
    k_ids = [jnp.max(k[rows:, :HD].astype(jnp.float32)) for k in ks]
    for i in range(4):
        for j in range(n_keys):

            @pl.when(k_ids[j] <= q_ids[i])
            def _():
                sums = None
                for h in range(heads):
                    cols = slice(h * HD, (h + 1) * HD)
                    scores = lax.dot_general(
                        qs[i][:rows, cols], ks[j][:rows, cols], (((1,), (1,)), ((), ())),
                        preferred_element_type=jnp.float32,
                    )
                    weights = jnp.exp2(scores).astype(jnp.bfloat16)
                    wide = jnp.concatenate([vs[j][:rows, cols], ones], axis=1)
                    both = jnp.dot(weights, wide, preferred_element_type=jnp.float32)
                    acc_ref[i, :, cols] += both[:, :HD]
                    sums = both[:, HD:] if h == 0 else jnp.where(lane == h, both[:, HD:], sums)
                acc_ref[i, :, heads * HD :] += sums
    if last:
        for n, i in enumerate((0, 2)):
            keep_ref[n] = acc_ref[i, :, : heads * HD]
            keep_sum[n] = acc_ref[i, :, heads * HD :].T[:8]
        for n, i in enumerate((1, 3)):
            write_share(send_ref.at[n], acc_ref[i, :, : heads * HD], acc_ref[i, :, heads * HD :].T[:8])


def write_share(ref, sums, totals):
    rows = sums.shape[0]
    ref[:rows] = sums.astype(jnp.bfloat16)
    pad = jnp.zeros((8, sums.shape[1] - rows), jnp.float32)
    high = totals.astype(jnp.bfloat16).astype(jnp.float32)
    low = totals - high
    both = jnp.concatenate(
        [jnp.concatenate([high, pad], axis=1), jnp.concatenate([low, pad], axis=1)], axis=0
    )
    ref[rows:] = both.astype(jnp.bfloat16)


def read_totals(ref, rows):
    both = ref[rows:, :rows].astype(jnp.float32)
    return both[:8] + both[8:]


def attend(qs, ks, vs, state, last):
    rows, width = qs[0].shape[0] - ID_ROWS, vs[0].shape[1]
    n_keys = len(ks)
    wide = width + HD
    vmem = pl.BlockSpec(memory_space=pltpu.VMEM)
    state_shape = jax.ShapeDtypeStruct((4, rows, wide), jnp.float32)
    if last:
        out_shape = [
            jax.ShapeDtypeStruct((2, rows, width), jnp.float32),
            jax.ShapeDtypeStruct((2, 8, rows), jnp.float32),
            jax.ShapeDtypeStruct((2, rows + ID_ROWS, width), jnp.bfloat16),
        ]
        scratch = [pltpu.VMEM((4, rows, wide), jnp.float32)]
    else:
        out_shape, scratch = [state_shape], []
    first = state is None
    args = [*qs, *ks, *vs] + ([] if first else [state])

    def body(*refs):
        attend_kernel(n_keys, first, last, *refs)

    flops = 4 * n_keys * 3 * rows * rows * HD * 4
    return pl.pallas_call(
        body,
        in_specs=[vmem] * len(args),
        out_specs=[vmem] * len(out_shape),
        out_shape=out_shape,
        scratch_shapes=scratch,
        compiler_params=pltpu.CompilerParams(vmem_limit_bytes=32 * MIB),
        cost_estimate=pl.CostEstimate(
            flops=flops, bytes_accessed=8 * MIB, transcendentals=4 * n_keys * 3 * rows * rows
        ),
        name="attend",
    )(*args)


def fold_kernel(keep_ref, sum_ref, got_ref, own_ref, own_sum, send_ref):
    rows = keep_ref.shape[1]
    own_ref[...] = keep_ref[0] + got_ref[0, :rows].astype(jnp.float32)
    own_sum[...] = sum_ref[0] + read_totals(got_ref.at[0], rows)
    write_share(
        send_ref,
        keep_ref[1] + got_ref[1, :rows].astype(jnp.float32),
        sum_ref[1] + read_totals(got_ref.at[1], rows),
    )


def fold(keep, sums, got):
    _, rows, width = keep.shape
    vmem = pl.BlockSpec(memory_space=pltpu.VMEM)
    return pl.pallas_call(
        fold_kernel,
        in_specs=[vmem] * 3,
        out_specs=[vmem] * 3,
        out_shape=[
            jax.ShapeDtypeStruct((rows, width), jnp.float32),
            jax.ShapeDtypeStruct((8, rows), jnp.float32),
            jax.ShapeDtypeStruct((rows + ID_ROWS, width), jnp.bfloat16),
        ],
        compiler_params=pltpu.CompilerParams(vmem_limit_bytes=8 * MIB),
        name="fold",
    )(keep, sums, got)


def finish_kernel(own_ref, sum_ref, got_ref, upper_ref, lower_ref):
    half, width = upper_ref.shape
    rows = 2 * half
    total = own_ref[...] + got_ref[:rows].astype(jnp.float32)
    sums = sum_ref[...] + read_totals(got_ref, rows)
    columns = jnp.concatenate([sums, jnp.ones((120, rows), jnp.float32)], axis=0).T
    for h in range(width // HD):
        cols = slice(h * HD, (h + 1) * HD)
        normed = (total[:, cols] / columns[:, h : h + 1]).astype(jnp.bfloat16)
        upper_ref[:, cols] = normed[:half]
        lower_ref[:, cols] = normed[half:]


def finish(own, sums, got):
    rows, width = own.shape
    vmem = pl.BlockSpec(memory_space=pltpu.VMEM)
    half = jax.ShapeDtypeStruct((rows // 2, width), jnp.bfloat16)
    return pl.pallas_call(
        finish_kernel,
        in_specs=[vmem] * 3,
        out_specs=[vmem] * 2,
        out_shape=[half, half],
        compiler_params=pltpu.CompilerParams(vmem_limit_bytes=8 * MIB),
        name="finish",
    )(own, sums, got)


def arrange_kernel(place_ref, own_ref, mate_ref, out_ref):
    c = place_ref[8]
    y_lo, z, core = c // 16, lax.rem(c // 2, N_Z), lax.rem(c, 2)
    for r in range(8):
        distance = lax.rem(place_ref[r] - z + N_Z, N_Z)
        slot = 0
        for d, held in enumerate(RING_SLOT):
            slot = jnp.where(distance == d, held, slot)
        for n in range(4):
            held, far = (own_ref, mate_ref)[n // 2], n % 2
            part = lax.rem(core + n // 2, 2) * 2 + lax.rem(y_lo + far, 2)
            out_ref[r, part] = held[far * 8 + slot]


def arrange_weight(own, mate, places):
    _, cols, width = own.shape
    vmem = pl.BlockSpec(memory_space=pltpu.VMEM)
    return pl.pallas_call(
        arrange_kernel,
        in_specs=[pl.BlockSpec(memory_space=pltpu.SMEM)] + [vmem] * 2,
        out_specs=vmem,
        out_shape=jax.ShapeDtypeStruct((8, 4, cols, width), own.dtype),
        compiler_params=pltpu.CompilerParams(vmem_limit_bytes=16 * MIB),
        cost_estimate=pl.CostEstimate(flops=0, bytes_accessed=8 * MIB, transcendentals=0),
        name="arrange",
    )(places, own, mate)


HERE, THERE = (0, 1, 2, 3), (4, 5, 6, 7)


def term_of(rows, w_ref, r):
    weight = w_ref[r].reshape(-1, rows.shape[1])
    return lax.dot_general(rows, weight, (((1,), (1,)), ((), ())), preferred_element_type=jnp.float32)


def project_first_kernel(b0, along, w_ref, upper_ref, lower_ref):
    half = upper_ref.shape[0]
    upper_ref[...] = term_of(b0[:half], w_ref, HERE[0]) + term_of(b0[half:], w_ref, THERE[0])
    lower = term_of(along[:half], w_ref, HERE[0])
    for n in range(1, 4):
        lower = lower + term_of(along[n * half : (n + 1) * half], w_ref, HERE[n])
    lower_ref[...] = lower


def project_kernel(b1, b2, b3, first_ref, w_ref, upper_ref):
    half = upper_ref.shape[0]
    upper = first_ref[...]
    for n, both in enumerate((b1, b2, b3)):
        for rows, r in ((both[:half], HERE[n + 1]), (both[half:], THERE[n + 1])):
            upper = upper + term_of(rows, w_ref, r)
    upper_ref[...] = upper.astype(jnp.bfloat16)


def project_last_kernel(upper_ref, lower_ref, far, w_ref, out_ref):
    half = upper_ref.shape[0]
    out_ref[:half] = upper_ref[...]
    lower = lower_ref[...]
    for n in range(4):
        lower = lower + term_of(far[n * half : (n + 1) * half], w_ref, THERE[n])
    out_ref[half:] = lower.astype(jnp.bfloat16)


def project(both, along, far, weight):
    rows, width = both[0].shape
    half = rows // 2
    columns = weight.shape[1] * weight.shape[2]
    vmem = pl.BlockSpec(memory_space=pltpu.VMEM)

    def call(kernel, args, out_shape, terms):
        return pl.pallas_call(
            kernel,
            in_specs=[vmem] * len(args),
            out_specs=[vmem] * len(out_shape),
            out_shape=out_shape,
            compiler_params=pltpu.CompilerParams(vmem_limit_bytes=16 * MIB),
            cost_estimate=pl.CostEstimate(
                flops=2 * half * terms * width * columns, bytes_accessed=8 * width * columns * 2, transcendentals=0
            ),
            name="project",
        )(*args)

    part = jax.ShapeDtypeStruct((half, columns), jnp.float32)
    upper, lower = call(project_first_kernel, [both[0], along, weight], [part, part], 6)
    (upper,) = call(
        project_kernel,
        [*both[1:], upper, weight],
        [jax.ShapeDtypeStruct((half, columns), jnp.bfloat16)],
        6,
    )
    return call(
        project_last_kernel,
        [upper, lower, far, weight],
        [jax.ShapeDtypeStruct((rows, columns), jnp.bfloat16)],
        4,
    )[0]


RING_SLOT = (0, 2, 5, 7, 3, 6, 4, 1)


def regroup_weight(out_weight):
    pairs = []
    for c in range(N_CTX):
        c_lo, c_z, c_core = c // 16, (c // 2) % N_Z, c % 2
        for t in range(N_TP):
            pairs.append(((4 * t + c_core * 2 + c_lo) * N_TP + c_z, c * N_TP + t))
    return lax.ppermute(out_weight.T, ("ctx", "tp"), pairs)


def on_device(tokens, qkv_weight, query_gain, key_gain, out_weight, block_ids):
    places = sender_places()
    out_block = regroup_weight(out_weight)
    half = tokens.shape[0] // 2
    weight = order_weight(qkv_weight.transpose(1, 0, 2), places)
    q_flat, k_flat, values, squares = qkv(
        *gather_tp(tokens[:half], tokens[half:]), weight, out_block
    )

    pair_sum = squares + move(squares, y_hi=1)
    tied = after(values, pair_sum)
    v_up, v_down = [values, move(tied, z=1)], [values, move(tied, z=-1)]
    parts = [pair_sum] + [move(pair_sum, x=x) for x in (2, 1, 3)]
    queries, keys = norm(
        block_ids, parts, after(q_flat, v_up[1], v_down[1]), k_flat, query_gain.reshape(1, -1), key_gain.reshape(1, -1)
    )

    k_up, k_down = [keys, move(keys, z=1)], [keys, move(keys, z=-1)]
    across = move(queries, y_lo=1)
    mate = move(after(queries, k_up[1]), core=1)
    qs = [queries, mate, across, move(across, core=1)]

    rows = block_ids.shape[0]
    for _ in range(2):
        v_up.append(move(v_up[-1], z=1))
        v_down.append(move(v_down[-1], z=-1))
    v_far = move(v_down[3][:rows], z=-1)
    out_far = move(after(out_block, k_up[1], k_down[1]), z=4)
    first = jnp.stack([v[rows:] for v in (values, v_up[1], v_down[1])] + [out_far])
    middle = jnp.stack([v[rows:] for v in (v_up[2], v_down[2], v_up[3], v_down[3])])
    first_far = move(after(first, across), y_lo=1)
    middle_far = move(after(middle, first_far), y_lo=1)

    k_up.append(move(k_up[1], z=1))
    k_down.append(move(k_down[1], z=-1))
    (state,) = attend(qs, [keys, k_up[1], k_down[1]], [values, v_up[1], v_down[1]], None, False)
    k_up.append(move(after(k_up[2], state), z=1))
    k_down.append(move(after(k_down[2], state), z=-1))
    (state,) = attend(qs, [k_up[2], k_down[2]], [v_up[2], v_down[2]], state, False)
    k_far = move(after(k_up[3], state), z=1)
    (state,) = attend(qs, [k_up[3], k_down[3]], [v_up[3], v_down[3]], state, False)
    keep, sums, send = attend(qs, [k_far], [v_far], state, True)

    own, sums, send = fold(keep, sums, move(send, core=1))
    got = move(send, y_lo=1)
    out_own = jnp.concatenate([first, middle, first_far, middle_far])
    out_mate = move(after(out_own, got), core=1)
    upper, lower = finish(own, sums, got)
    both, along, far = gather_tp(upper, lower)
    out_whole = arrange_weight(out_own, out_mate, places)
    return project(both, along, far, out_whole)


def solution(mesh):
    in_specs = (P("ctx", "tp"), P(None, None, "tp"), P("tp"), P("tp"), P("tp", "ctx"), P("ctx"))
    out_specs = P("ctx", "tp")
    return jax.shard_map(
        on_device, mesh=mesh, in_specs=in_specs, out_specs=out_specs, check_vma=False
    )
```

```python
import math

import jax
import jax.numpy as jnp
from jax import lax
from jax.experimental import pallas as pl
from jax.experimental.pallas import tpu as pltpu
from jax.sharding import PartitionSpec as P

HEADS = 24
HD = 128
ID_ROWS = 16
N_Z = 8
N_X = 4
N_TP = 8
N_CTX = 32
MIB = 1 << 20


def move(value, x=0, y_hi=0, y_lo=0, z=0, core=0):
    pairs = []
    for c in range(N_CTX):
        for t in range(N_TP):
            c_lo, c_z, c_core = c // 16, (c // 2) % 8, c % 2
            t_x, t_hi = t // 2, t % 2
            dst_c = ((c_lo + y_lo) % 2) * 16 + ((c_z + z) % N_Z) * 2 + (c_core + core) % 2
            dst_t = ((t_x + x) % N_X) * 2 + (t_hi + y_hi) % 2
            pairs.append((c * N_TP + t, dst_c * N_TP + dst_t))
    return lax.ppermute(value, ("ctx", "tp"), pairs)


TP_STEPS = [(0, 0), (1, 0), (3, 0), (2, 0), (0, 1), (1, 1), (3, 1), (2, 1)]


def after(value, *others):
    return lax.optimization_barrier((value, *others))[0]


def gather_tp(upper, lower):
    both = jnp.concatenate([upper, move(upper, y_hi=1)])
    along = jnp.concatenate([lower] + [move(lower, x=x) for x in (1, 3, 2)])
    far = move(along, y_hi=1)
    return [both] + [move(both, x=x) for x in (1, 3, 2)], along, far


def sender_places():
    t = lax.axis_index("tp")
    t_x, t_hi = t // 2, t % 2
    places = [((t_x - x + N_X) % N_X) * 2 + (t_hi - y_hi + 2) % 2 for x, y_hi in TP_STEPS]
    return jnp.stack(places + [lax.axis_index("ctx")]).astype(jnp.int32)


def order_kernel(place_ref, w_ref, out_ref, sems):
    feats = out_ref.shape[1] // 8

    def fetch(r):
        start = pl.multiple_of(place_ref[r] * feats, feats)
        return pltpu.make_async_copy(
            w_ref.at[:, pl.ds(start, feats), :], out_ref.at[:, pl.ds(r * feats, feats), :], sems.at[r]
        )

    for r in range(8):
        fetch(r).start()
    for r in range(8):
        fetch(r).wait()


def order_weight(weight, places):
    return pl.pallas_call(
        order_kernel,
        in_specs=[pl.BlockSpec(memory_space=pltpu.SMEM), pl.BlockSpec(memory_space=pl.ANY)],
        out_specs=pl.BlockSpec(memory_space=pltpu.VMEM),
        out_shape=jax.ShapeDtypeStruct(weight.shape, weight.dtype),
        scratch_shapes=[pltpu.SemaphoreType.DMA((8,))],
        compiler_params=pltpu.CompilerParams(vmem_limit_bytes=32 * MIB),
        cost_estimate=pl.CostEstimate(flops=0, bytes_accessed=24 * MIB, transcendentals=0),
        name="order",
    )(places, weight)


def product(rows, w_ref, p, block):
    wide = jnp.concatenate(rows, axis=1) if len(rows) > 1 else rows[0]
    feats = w_ref.shape[1] // 8
    return jnp.dot(
        wide, w_ref[p, block * feats : block * feats + wide.shape[1], :], preferred_element_type=jnp.float32
    )


def lower_kernel(block, *refs):
    held, w_ref, out_ref = refs[0], refs[-2], refs[-1]
    half = held.shape[0] // 4
    rows = [held[n * half : (n + 1) * half] for n in range(4)]
    for p in range(3):
        term = product(rows, w_ref, p, block)
        out_ref[p] = term if block == 0 else refs[1][p] + term


def upper_kernel(b0, b1, b2, w_ref, out_ref):
    half = b0.shape[0] // 2
    for p in range(3):
        here = product([b[:half] for b in (b0, b1, b2)], w_ref, p, 0)
        out_ref[p] = here + product([b[half:] for b in (b0, b1, b2)], w_ref, p, 4)


def last_kernel(b3, upper_ref, lower_ref, w_ref, out_w, q_ref, k_ref, v_ref, sq_ref):
    half = b3.shape[0] // 2

    def whole(p):
        upper = upper_ref[p] + product([b3[:half]], w_ref, p, 3) + product([b3[half:]], w_ref, p, 7)
        return jnp.concatenate([upper, lower_ref[p]], axis=0)

    q, k, v = [whole(p) for p in range(3)]
    q_ref[...] = q
    k_ref[...] = k
    v_ref[: v.shape[0]] = v.astype(jnp.bfloat16)
    v_ref[v.shape[0] :] = out_w[...]
    q_sq = jnp.sum(q * q, axis=1, keepdims=True)
    k_sq = jnp.sum(k * k, axis=1, keepdims=True)
    lane = lax.broadcasted_iota(jnp.int32, (q.shape[0], 128), 1)
    both = jnp.where(lane == 0, q_sq, jnp.where(lane == 1, k_sq, 0.0))
    sq_ref[...] = both.T[:8]


def qkv(firsts, along, far, weight, out_block):
    rows, feats = firsts[0].shape
    half = rows // 2
    width = weight.shape[2]
    vmem = pl.BlockSpec(memory_space=pltpu.VMEM)
    share = jax.ShapeDtypeStruct((3, half, width), jnp.float32)

    def call(kernel, args, out_shape, blocks):
        return pl.pallas_call(
            kernel,
            in_specs=[vmem] * len(args),
            out_specs=[vmem] * len(out_shape),
            out_shape=out_shape,
            compiler_params=pltpu.CompilerParams(vmem_limit_bytes=32 * MIB),
            cost_estimate=pl.CostEstimate(
                flops=2 * half * blocks * feats * 3 * width,
                bytes_accessed=blocks * feats * 3 * width * 2,
                transcendentals=0,
            ),
            name="qkv",
        )(*args)

    def lower_part(block, *args):
        return call(lambda *refs: lower_kernel(block, *refs), [*args, weight], [share], 4)[0]

    lower = lower_part(0, along)
    lower = lower_part(4, far, lower)
    (upper,) = call(upper_kernel, [*firsts[:3], weight], [share], 6)
    whole = jax.ShapeDtypeStruct((rows, width), jnp.float32)
    return call(
        last_kernel,
        [firsts[3], upper, lower, weight, out_block],
        [
            whole,
            whole,
            jax.ShapeDtypeStruct((rows + out_block.shape[0], width), jnp.bfloat16),
            jax.ShapeDtypeStruct((8, rows), jnp.float32),
        ],
        2,
    )


def norm_kernel(id_ref, s0, s1, s2, s3, q_ref, k_ref, qg_ref, kg_ref, q_out, k_out):
    rows = q_ref.shape[0]
    total = s0[...] + s1[...] + s2[...] + s3[...]
    inverse = lax.rsqrt(total * (1.0 / (HEADS * HD)) + 1e-06)
    columns = jnp.concatenate([inverse, jnp.zeros((120, rows), jnp.float32)], axis=0).T
    q_scale = math.log2(math.e) / math.sqrt(HD)
    q_out[:rows] = (q_ref[...] * columns[:, 0:1] * (qg_ref[...] * q_scale)).astype(jnp.bfloat16)
    k_out[:rows] = (k_ref[...] * columns[:, 1:2] * kg_ref[...]).astype(jnp.bfloat16)
    span = jnp.full((ID_ROWS, q_ref.shape[1]), id_ref[0].astype(jnp.float32), jnp.float32)
    q_out[rows:] = span.astype(jnp.bfloat16)
    k_out[rows:] = span.astype(jnp.bfloat16)


def norm(span_id, squares, q, k, q_gain, k_gain):
    rows, width = q.shape
    vmem = pl.BlockSpec(memory_space=pltpu.VMEM)
    out = jax.ShapeDtypeStruct((rows + ID_ROWS, width), jnp.bfloat16)
    return pl.pallas_call(
        norm_kernel,
        in_specs=[pl.BlockSpec(memory_space=pltpu.SMEM)] + [vmem] * 8,
        out_specs=[vmem] * 2,
        out_shape=[out, out],
        compiler_params=pltpu.CompilerParams(vmem_limit_bytes=12 * MIB),
        name="norm",
    )(span_id, *squares, q, k, q_gain, k_gain)


def attend_kernel(n_keys, first, last, *refs):
    qs, ks, vs = refs[:4], refs[4 : 4 + n_keys], refs[4 + n_keys : 4 + 2 * n_keys]
    rest = refs[4 + 2 * n_keys :]
    rows = qs[0].shape[0] - ID_ROWS
    heads = vs[0].shape[1] // HD
    if first:
        acc_ref, = rest[:1]
        acc_ref[...] = jnp.zeros_like(acc_ref)
    elif last:
        acc_in, keep_ref, keep_sum, send_ref, acc_ref = rest
        acc_ref[...] = acc_in[...]
    else:
        acc_in, acc_ref = rest
        acc_ref[...] = acc_in[...]
    lane = lax.broadcasted_iota(jnp.int32, (rows, HD), 1)
    ones = jnp.ones((rows, HD), jnp.bfloat16)
    q_ids = [jnp.max(q[rows:, :HD].astype(jnp.float32)) for q in qs]
    k_ids = [jnp.max(k[rows:, :HD].astype(jnp.float32)) for k in ks]
    for i in range(4):
        for j in range(n_keys):

            @pl.when(k_ids[j] <= q_ids[i])
            def _():
                sums = None
                for h in range(heads):
                    cols = slice(h * HD, (h + 1) * HD)
                    scores = lax.dot_general(
                        qs[i][:rows, cols], ks[j][:rows, cols], (((1,), (1,)), ((), ())),
                        preferred_element_type=jnp.float32,
                    )
                    weights = jnp.exp2(scores).astype(jnp.bfloat16)
                    wide = jnp.concatenate([vs[j][:rows, cols], ones], axis=1)
                    both = jnp.dot(weights, wide, preferred_element_type=jnp.float32)
                    acc_ref[i, :, cols] += both[:, :HD]
                    sums = both[:, HD:] if h == 0 else jnp.where(lane == h, both[:, HD:], sums)
                acc_ref[i, :, heads * HD :] += sums
    if last:
        for n, i in enumerate((0, 2)):
            keep_ref[n] = acc_ref[i, :, : heads * HD]
            keep_sum[n] = acc_ref[i, :, heads * HD :].T[:8]
        for n, i in enumerate((1, 3)):
            write_share(send_ref.at[n], acc_ref[i, :, : heads * HD], acc_ref[i, :, heads * HD :].T[:8])


def write_share(ref, sums, totals):
    rows = sums.shape[0]
    ref[:rows] = sums.astype(jnp.bfloat16)
    pad = jnp.zeros((8, sums.shape[1] - rows), jnp.float32)
    high = totals.astype(jnp.bfloat16).astype(jnp.float32)
    low = totals - high
    both = jnp.concatenate(
        [jnp.concatenate([high, pad], axis=1), jnp.concatenate([low, pad], axis=1)], axis=0
    )
    ref[rows:] = both.astype(jnp.bfloat16)


def read_totals(ref, rows):
    both = ref[rows:, :rows].astype(jnp.float32)
    return both[:8] + both[8:]


def attend(qs, ks, vs, state, last):
    rows, width = qs[0].shape[0] - ID_ROWS, vs[0].shape[1]
    n_keys = len(ks)
    wide = width + HD
    vmem = pl.BlockSpec(memory_space=pltpu.VMEM)
    state_shape = jax.ShapeDtypeStruct((4, rows, wide), jnp.float32)
    if last:
        out_shape = [
            jax.ShapeDtypeStruct((2, rows, width), jnp.float32),
            jax.ShapeDtypeStruct((2, 8, rows), jnp.float32),
            jax.ShapeDtypeStruct((2, rows + ID_ROWS, width), jnp.bfloat16),
        ]
        scratch = [pltpu.VMEM((4, rows, wide), jnp.float32)]
    else:
        out_shape, scratch = [state_shape], []
    first = state is None
    args = [*qs, *ks, *vs] + ([] if first else [state])

    def body(*refs):
        attend_kernel(n_keys, first, last, *refs)

    flops = 4 * n_keys * 3 * rows * rows * HD * 4
    return pl.pallas_call(
        body,
        in_specs=[vmem] * len(args),
        out_specs=[vmem] * len(out_shape),
        out_shape=out_shape,
        scratch_shapes=scratch,
        compiler_params=pltpu.CompilerParams(vmem_limit_bytes=32 * MIB),
        cost_estimate=pl.CostEstimate(
            flops=flops, bytes_accessed=8 * MIB, transcendentals=4 * n_keys * 3 * rows * rows
        ),
        name="attend",
    )(*args)


def fold_kernel(keep_ref, sum_ref, got_ref, own_ref, own_sum, send_ref):
    rows = keep_ref.shape[1]
    own_ref[...] = keep_ref[0] + got_ref[0, :rows].astype(jnp.float32)
    own_sum[...] = sum_ref[0] + read_totals(got_ref.at[0], rows)
    write_share(
        send_ref,
        keep_ref[1] + got_ref[1, :rows].astype(jnp.float32),
        sum_ref[1] + read_totals(got_ref.at[1], rows),
    )


def fold(keep, sums, got):
    _, rows, width = keep.shape
    vmem = pl.BlockSpec(memory_space=pltpu.VMEM)
    return pl.pallas_call(
        fold_kernel,
        in_specs=[vmem] * 3,
        out_specs=[vmem] * 3,
        out_shape=[
            jax.ShapeDtypeStruct((rows, width), jnp.float32),
            jax.ShapeDtypeStruct((8, rows), jnp.float32),
            jax.ShapeDtypeStruct((rows + ID_ROWS, width), jnp.bfloat16),
        ],
        compiler_params=pltpu.CompilerParams(vmem_limit_bytes=8 * MIB),
        name="fold",
    )(keep, sums, got)


def finish_kernel(own_ref, sum_ref, got_ref, upper_ref, lower_ref):
    half, width = upper_ref.shape
    rows = 2 * half
    total = own_ref[...] + got_ref[:rows].astype(jnp.float32)
    sums = sum_ref[...] + read_totals(got_ref, rows)
    columns = jnp.concatenate([sums, jnp.ones((120, rows), jnp.float32)], axis=0).T
    for h in range(width // HD):
        cols = slice(h * HD, (h + 1) * HD)
        normed = (total[:, cols] / columns[:, h : h + 1]).astype(jnp.bfloat16)
        upper_ref[:, cols] = normed[:half]
        lower_ref[:, cols] = normed[half:]


def finish(own, sums, got):
    rows, width = own.shape
    vmem = pl.BlockSpec(memory_space=pltpu.VMEM)
    half = jax.ShapeDtypeStruct((rows // 2, width), jnp.bfloat16)
    return pl.pallas_call(
        finish_kernel,
        in_specs=[vmem] * 3,
        out_specs=[vmem] * 2,
        out_shape=[half, half],
        compiler_params=pltpu.CompilerParams(vmem_limit_bytes=8 * MIB),
        name="finish",
    )(own, sums, got)


def arrange_kernel(place_ref, own_ref, mate_ref, out_ref):
    c = place_ref[8]
    y_lo, z, core = c // 16, lax.rem(c // 2, N_Z), lax.rem(c, 2)
    for r in range(8):
        distance = lax.rem(place_ref[r] - z + N_Z, N_Z)
        slot = 0
        for d, held in enumerate(RING_SLOT):
            slot = jnp.where(distance == d, held, slot)
        for n in range(4):
            held, far = (own_ref, mate_ref)[n // 2], n % 2
            part = lax.rem(core + n // 2, 2) * 2 + lax.rem(y_lo + far, 2)
            out_ref[r, part] = held[far * 8 + slot]


def arrange_weight(own, mate, places):
    _, cols, width = own.shape
    vmem = pl.BlockSpec(memory_space=pltpu.VMEM)
    return pl.pallas_call(
        arrange_kernel,
        in_specs=[pl.BlockSpec(memory_space=pltpu.SMEM)] + [vmem] * 2,
        out_specs=vmem,
        out_shape=jax.ShapeDtypeStruct((8, 4, cols, width), own.dtype),
        compiler_params=pltpu.CompilerParams(vmem_limit_bytes=16 * MIB),
        cost_estimate=pl.CostEstimate(flops=0, bytes_accessed=8 * MIB, transcendentals=0),
        name="arrange",
    )(places, own, mate)


HERE, THERE = (0, 1, 2, 3), (4, 5, 6, 7)


def term_of(rows, w_ref, r):
    weight = w_ref[r].reshape(-1, rows.shape[1])
    return lax.dot_general(rows, weight, (((1,), (1,)), ((), ())), preferred_element_type=jnp.float32)


def project_first_kernel(b0, along, w_ref, upper_ref, lower_ref):
    half = upper_ref.shape[0]
    upper_ref[...] = term_of(b0[:half], w_ref, HERE[0]) + term_of(b0[half:], w_ref, THERE[0])
    lower = term_of(along[:half], w_ref, HERE[0])
    for n in range(1, 4):
        lower = lower + term_of(along[n * half : (n + 1) * half], w_ref, HERE[n])
    lower_ref[...] = lower


def project_kernel(b1, b2, b3, first_ref, w_ref, upper_ref):
    half = upper_ref.shape[0]
    upper = first_ref[...]
    for n, both in enumerate((b1, b2, b3)):
        for rows, r in ((both[:half], HERE[n + 1]), (both[half:], THERE[n + 1])):
            upper = upper + term_of(rows, w_ref, r)
    upper_ref[...] = upper.astype(jnp.bfloat16)


def project_last_kernel(upper_ref, lower_ref, far, w_ref, out_ref):
    half = upper_ref.shape[0]
    out_ref[:half] = upper_ref[...]
    lower = lower_ref[...]
    for n in range(4):
        lower = lower + term_of(far[n * half : (n + 1) * half], w_ref, THERE[n])
    out_ref[half:] = lower.astype(jnp.bfloat16)


def project(both, along, far, weight):
    rows, width = both[0].shape
    half = rows // 2
    columns = weight.shape[1] * weight.shape[2]
    vmem = pl.BlockSpec(memory_space=pltpu.VMEM)

    def call(kernel, args, out_shape, terms):
        return pl.pallas_call(
            kernel,
            in_specs=[vmem] * len(args),
            out_specs=[vmem] * len(out_shape),
            out_shape=out_shape,
            compiler_params=pltpu.CompilerParams(vmem_limit_bytes=16 * MIB),
            cost_estimate=pl.CostEstimate(
                flops=2 * half * terms * width * columns, bytes_accessed=8 * width * columns * 2, transcendentals=0
            ),
            name="project",
        )(*args)

    part = jax.ShapeDtypeStruct((half, columns), jnp.float32)
    upper, lower = call(project_first_kernel, [both[0], along, weight], [part, part], 6)
    (upper,) = call(
        project_kernel,
        [*both[1:], upper, weight],
        [jax.ShapeDtypeStruct((half, columns), jnp.bfloat16)],
        6,
    )
    return call(
        project_last_kernel,
        [upper, lower, far, weight],
        [jax.ShapeDtypeStruct((rows, columns), jnp.bfloat16)],
        4,
    )[0]


RING_SLOT = (0, 2, 4, 6, 7, 5, 3, 1)


def regroup_weight(out_weight):
    pairs = []
    for c in range(N_CTX):
        c_lo, c_z, c_core = c // 16, (c // 2) % N_Z, c % 2
        for t in range(N_TP):
            pairs.append(((4 * t + c_core * 2 + c_lo) * N_TP + c_z, c * N_TP + t))
    return lax.ppermute(out_weight.T, ("ctx", "tp"), pairs)


def on_device(tokens, qkv_weight, query_gain, key_gain, out_weight, block_ids):
    places = sender_places()
    out_block = regroup_weight(out_weight)
    half = tokens.shape[0] // 2
    weight = order_weight(qkv_weight.transpose(1, 0, 2), places)
    q_flat, k_flat, values, squares = qkv(
        *gather_tp(tokens[:half], tokens[half:]), weight, out_block
    )

    pair_sum = squares + move(squares, y_hi=1)
    tied = after(values, pair_sum)
    v_up, v_down = [values, move(tied, z=1)], [values, move(tied, z=-1)]
    parts = [pair_sum] + [move(pair_sum, x=x) for x in (2, 1, 3)]
    queries, keys = norm(
        block_ids, parts, after(q_flat, v_up[1], v_down[1]), k_flat, query_gain.reshape(1, -1), key_gain.reshape(1, -1)
    )

    k_up, k_down = [keys, move(keys, z=1)], [keys, move(keys, z=-1)]
    across = move(queries, y_lo=1)
    mate = move(after(queries, k_up[1]), core=1)
    qs = [queries, mate, across, move(across, core=1)]

    rows = block_ids.shape[0]
    for _ in range(2):
        v_up.append(move(v_up[-1], z=1))
        v_down.append(move(v_down[-1], z=-1))
    v_far = move(v_down[3], z=-1)
    first = jnp.stack([v[rows:] for v in (values, v_up[1], v_down[1])])
    middle = jnp.stack([v[rows:] for v in (v_up[2], v_down[2], v_up[3], v_down[3])])
    first_far, middle_far = move(after(first, across, k_up[1], k_down[1]), y_lo=1), move(middle, y_lo=1)

    k_up.append(move(k_up[1], z=1))
    k_down.append(move(k_down[1], z=-1))
    (state,) = attend(qs, [keys, k_up[1], k_down[1]], [values, v_up[1], v_down[1]], None, False)
    k_up.append(move(after(k_up[2], state), z=1))
    k_down.append(move(after(k_down[2], state), z=-1))
    (state,) = attend(qs, [k_up[2], k_down[2]], [v_up[2], v_down[2]], state, False)
    k_far = move(after(k_up[3], state), z=1)
    (state,) = attend(qs, [k_up[3], k_down[3]], [v_up[3], v_down[3]], state, False)
    keep, sums, send = attend(qs, [k_far], [v_far], state, True)

    own, sums, send = fold(keep, sums, move(send, core=1))
    got = move(send, y_lo=1)
    late = v_far[None, rows:]
    out_own = jnp.concatenate([first, middle, late, first_far, middle_far, move(late, y_lo=1)])
    out_mate = move(after(out_own, got), core=1)
    upper, lower = finish(own, sums, got)
    both, along, far = gather_tp(upper, lower)
    out_whole = arrange_weight(out_own, out_mate, places)
    return project(both, along, far, out_whole)


def solution(mesh):
    in_specs = (P("ctx", "tp"), P(None, None, "tp"), P("tp"), P("tp"), P("tp", "ctx"), P("ctx"))
    out_specs = P("ctx", "tp")
    return jax.shard_map(
        on_device, mesh=mesh, in_specs=in_specs, out_specs=out_specs, check_vma=False
    )
```
